32 devices in a mesh: rep: 2 (over y), inst: 4 (over z), tp: 4 (over x, core).
Axes of the slice: x: 2, y: 2, z: 4, core: 2. Of those that a mesh axis runs over, the one named last changes fastest.
Arguments:
- dest_slot: int32 [112], P('rep'), parts along dimension 0, may hold values from 0 to 55, as said below
- finished: int32 [112], P(('rep', 'inst')), parts along dimension 0, may hold values from 0 to 1, as said below
- lengths: int32 [112], P(('rep', 'inst')), parts along dimension 0, may hold values from 1 to 128
- cache_keys: bfloat16 [112, 256, 1024], P(('rep', 'inst'), None, 'tp'), parts along dimension 0, may hold values from -6 to 6
- cache_values: bfloat16 [112, 256, 1024], P(('rep', 'inst'), None, 'tp'), parts along dimension 0, may hold values from -6 to 6
- responses: bfloat16 [112, 128, 3072], P(('rep', 'inst'), None, 'tp'), parts along dimension 0, may hold values from -6 to 6
- dec_queries: bfloat16 [112, 2, 4096], P(('rep', 'inst'), None, 'tp'), parts along dimension 0, may hold values from -6 to 6
- new_keys: bfloat16 [112, 2, 1024], P(('rep', 'inst'), None, 'tp'), parts along dimension 0, may hold values from -6 to 6
- new_values: bfloat16 [112, 2, 1024], P(('rep', 'inst'), None, 'tp'), parts along dimension 0, may hold values from -6 to 6
- norm_gain: float32 [3072], replicated, may hold values from 0.5 to 2
- w_query: bfloat16 [3072, 4096], P(None, 'tp'), may hold values from -0.108253175 to 0.108253175
- w_key: bfloat16 [3072, 1024], P(None, 'tp'), may hold values from -0.108253175 to 0.108253175
- w_value: bfloat16 [3072, 1024], P(None, 'tp'), may hold values from -0.109375 to 0.109375
- w_out: bfloat16 [4096, 3072], P('tp'), may hold values from -0.09375 to 0.09375
Outputs:
- decode_out: bfloat16 [112, 2, 4096], P(('rep', 'inst'), None, 'tp'), parts along dimension 0
- prefill_out: bfloat16 [112, 128, 3072], P(('rep', 'inst'), None, 'tp'), parts along dimension 0
The draws below stay inside these ranges and needn't reach their ends.
There are 2 independent parts, one for each index of `rep`. The reference program is written for one: setup_inputs(seed, part) draws one part's arguments, and reference() takes and returns one part's arrays. A program takes and returns all parts, laid end to end along the dimension named above; an argument that names none is the same for every part. Nothing has to cross between parts.
Inputs may be any that keep to these rules, and one draw needn't show every extreme that they name: `dest_slot`: A permutation of the slots; slot s lies on instance s // 14. Row j of instance i goes to instance (i + a shift that depends on j only) mod 4; every shift used is used by exactly 7 values of j, so each instance sends its rows in groups of 7 to 2 distinct instances, and each instance receives 14 rows. The shifts used are 1 and 2. The rows that one instance receives are all unfinished or all finished; exactly 1 instance receives unfinished rows.
All inputs are finite; a program needn't handle non-finite values.
Results may differ from the reference program's by a relative error of at most 0.011.
Values may be sent and summed in bfloat16 or wider, within the bound.
No kernel may reach another device: no remote copies, remote signals or barrier semaphores. Data moves between devices by JAX's collectives and lax.ppermute only.
A program may use at most 128 MiB of HBM per device.

```python
import math
import jax
import jax.numpy as jnp
from jax import lax

D = 3072
QH = 32
KVH = 8
HD = 128
ROWS = 14
RESP = 128
PROMPT = 128
STEPS = 2
CAP = 7
CACHE = 256
SLOTS = 56
DEC_INST = 1
N_INST = 4
N_TP = 4


def routing(key):
    inst_count = N_INST
    order_key, pair_key, slot_key, pick_key = jax.random.split(key, 4)
    values = jnp.arange(inst_count, dtype=jnp.int32)
    forced = (values == 1) | (values == inst_count // 2) | (values == inst_count - 1)
    shuffled = jax.random.permutation(order_key, inst_count).astype(jnp.int32)
    position = jnp.zeros((inst_count,), jnp.int32).at[shuffled].set(values)
    priority = jnp.where(forced, values, inst_count + position)
    chosen = jnp.argsort(priority, stable=True)[:ROWS // CAP].astype(jnp.int32)
    shifts = jnp.repeat(chosen, CAP)[jax.random.permutation(pair_key, ROWS)]
    anchor = jnp.arange(inst_count, dtype=jnp.int32)[:, None]
    target = (anchor + shifts[None, :]) % inst_count
    slot_keys = jax.random.split(slot_key, inst_count)
    slot_table = jax.vmap(lambda entry_key: jax.random.permutation(entry_key, ROWS))(slot_keys).astype(jnp.int32)
    within = slot_table[target, jnp.arange(ROWS, dtype=jnp.int32)[None, :]]
    destination = (target * ROWS + within).reshape(-1).astype(jnp.int32)
    picked = jax.random.permutation(pick_key, inst_count)[:DEC_INST]
    decoding = jnp.zeros((inst_count,), jnp.int32).at[picked].set(1)
    flags = (1 - decoding[target]).reshape(-1).astype(jnp.int32)
    return (destination, flags)


def draw_dest_slot(key, part):
    destination, flags = routing(key)
    return destination


def draw_finished(key, part):
    destination, flags = routing(key)
    return flags


def draw_cache_keys(key, part):
    key = jax.random.fold_in(key, 17)
    return jnp.clip(jax.random.normal(key, (SLOTS, CACHE, KVH * HD), jnp.float32), -6.0, 6.0).astype(jnp.bfloat16)


def draw_dec_queries(key, part):
    key = jax.random.fold_in(key, 19)
    return jnp.clip(jax.random.normal(key, (SLOTS, STEPS, QH * HD), jnp.float32), -6.0, 6.0).astype(jnp.bfloat16)


def draw_responses(key, part):
    key = jax.random.fold_in(key, 29)
    return jnp.clip(jax.random.normal(key, (SLOTS, RESP, D), jnp.float32), -6.0, 6.0).astype(jnp.bfloat16)


def draw_norm_gain(key, part):
    key = jax.random.fold_in(key, 11)
    return jnp.exp(jax.random.uniform(key, (D,), jnp.float32, math.log(0.51), math.log(1.99)))


def draw_w_query(key, part):
    key = jax.random.fold_in(key, 13)
    scale = D ** (-0.5)
    return (jnp.clip(jax.random.normal(key, (D, QH * HD), jnp.float32), -5.9, 5.9) * scale).astype(jnp.bfloat16)


def draw_w_key(key, part):
    key = jax.random.fold_in(key, 23)
    scale = D ** (-0.5)
    return (jnp.clip(jax.random.normal(key, (D, KVH * HD), jnp.float32), -5.9, 5.9) * scale).astype(jnp.bfloat16)


def place_ends(array, rng, low, high):
    extent = array.shape
    spot = [jax.random.randint(jax.random.fold_in(rng, axis), (), 0, extent[axis]) for axis in range(len(extent))]
    array = array.at[tuple(spot)].set(low)
    longest = extent.index(max(extent))
    spot[longest] = (spot[longest] + 1) % extent[longest]
    return array.at[tuple(spot)].set(high)


def level_of(rng, dims, cuts, smallest, top_value):
    level, own = 1.0, jax.random.fold_in(rng, 6)
    for dim, shards_of in cuts:
        draws = jnp.exp(jax.random.uniform(jax.random.fold_in(own, dim), (shards_of,), jnp.float32, smallest / len(cuts), top_value / len(cuts)))
        level = level * jnp.repeat(draws, dims[dim] // shards_of).reshape([-1 if axis == dim else 1 for axis in range(len(dims))])
    return level


def scatter_about(stream_key, extent, scale, reach, shards=(), kind=jnp.bfloat16):
    level = level_of(stream_key, extent, shards, -0.22, 0.18) if shards else 1.0
    values = jax.random.normal(stream_key, extent, jnp.float32) * scale * level
    return jnp.minimum(jnp.maximum(values, -reach), reach).astype(kind)


def setup_inputs(seed: int = 0, part: int = 0) -> dict:
    key_of = jax.random.split(jax.random.key(seed), 15)
    part_splits = jax.random.split(jax.random.fold_in(key_of[14], part), 15)
    return {
        "dest_slot": draw_dest_slot(jax.random.fold_in(jax.random.fold_in(key_of[14], part), 71), part),
        "finished": draw_finished(jax.random.fold_in(jax.random.fold_in(key_of[14], part), 71), part),
        "lengths": place_ends(jax.random.randint(part_splits[2], (SLOTS,), 1, RESP + 1), jax.random.fold_in(part_splits[2], 1), 1, RESP).astype(jnp.int32),
        "cache_keys": draw_cache_keys(jax.random.fold_in(jax.random.fold_in(key_of[14], part), 71), part),
        "cache_values": scatter_about(part_splits[4], (SLOTS, CACHE, KVH * HD), 1.0, 6.0, ((0, 4), (2, 4))),
        "responses": draw_responses(jax.random.fold_in(jax.random.fold_in(key_of[14], part), 71), part),
        "dec_queries": draw_dec_queries(jax.random.fold_in(jax.random.fold_in(key_of[14], part), 71), part),
        "new_keys": scatter_about(part_splits[7], (SLOTS, STEPS, KVH * HD), 1.0, 6.0, ((0, 4), (2, 4))),
        "new_values": scatter_about(part_splits[8], (SLOTS, STEPS, KVH * HD), 1.0, 6.0, ((0, 4), (2, 4))),
        "norm_gain": draw_norm_gain(jax.random.fold_in(key_of[14], 71), part),
        "w_query": draw_w_query(jax.random.fold_in(key_of[14], 71), part),
        "w_key": draw_w_key(jax.random.fold_in(key_of[14], 71), part),
        "w_value": scatter_about(key_of[12], (D, KVH * HD), D ** -0.5, 0.109375, ((1, 4),)),
        "w_out": scatter_about(key_of[13], (QH * HD, D), (QH * HD) ** -0.5, 0.09375, ((0, 4),)),
    }


def decode_slot(queries, fresh_keys, fresh_values, old_keys, old_values, length):
    group_size = QH // KVH
    score_scale = 1.0 / math.sqrt(HD)
    query_heads = queries.astype(jnp.float32).reshape(STEPS, KVH, group_size, HD)
    key_heads = old_keys.astype(jnp.float32).reshape(CACHE, KVH, HD)
    value_heads = old_values.astype(jnp.float32).reshape(CACHE, KVH, HD)
    fresh_key_heads = fresh_keys.astype(jnp.float32).reshape(STEPS, KVH, HD)
    fresh_value_heads = fresh_values.astype(jnp.float32).reshape(STEPS, KVH, HD)
    old_scores = jnp.einsum('skgd,pkd->skgp', query_heads, key_heads) * score_scale
    new_scores = jnp.einsum('skgd,tkd->skgt', query_heads, fresh_key_heads) * score_scale
    old_valid = jnp.arange(CACHE)[None, None, None, :] < PROMPT + length
    step_index = jnp.arange(STEPS)
    new_valid = (step_index[None, :] <= step_index[:, None])[:, None, None, :]
    old_scores = jnp.where(old_valid, old_scores, -1e+30)
    new_scores = jnp.where(new_valid, new_scores, -1e+30)
    top_score = jnp.maximum(lax.optimization_barrier(jnp.max(old_scores, axis=-1, keepdims=True)), lax.optimization_barrier(jnp.max(new_scores, axis=-1, keepdims=True)))
    old_weights = jnp.exp(old_scores - top_score)
    new_weights = jnp.exp(new_scores - top_score)
    totals = lax.optimization_barrier(jnp.sum(old_weights, axis=-1, keepdims=True)) + lax.optimization_barrier(jnp.sum(new_weights, axis=-1, keepdims=True))
    old_probs = (old_weights / totals).astype(jnp.bfloat16)
    new_probs = (new_weights / totals).astype(jnp.bfloat16)
    mixed = jnp.einsum('skgp,pkd->skgd', old_probs.astype(jnp.float32), value_heads)
    mixed = mixed + jnp.einsum('skgt,tkd->skgd', new_probs.astype(jnp.float32), fresh_value_heads)
    return mixed.astype(jnp.bfloat16).reshape(STEPS, QH * HD)

def prefill_slot(states, length, norm_gain, w_query, w_key, w_value, w_out):
    group_size = QH // KVH
    score_scale = 1.0 / math.sqrt(HD)
    states_f = states.astype(jnp.float32)
    mean_square = lax.optimization_barrier(jnp.mean(states_f * states_f, axis=-1, keepdims=True))
    normed = (states_f * lax.rsqrt(mean_square + 1e-06) * norm_gain).astype(jnp.bfloat16)
    query_proj = jnp.dot(normed, w_query, preferred_element_type=jnp.float32).astype(jnp.bfloat16)
    key_proj = jnp.dot(normed, w_key, preferred_element_type=jnp.float32).astype(jnp.bfloat16)
    value_proj = jnp.dot(normed, w_value, preferred_element_type=jnp.float32).astype(jnp.bfloat16)
    query_heads = query_proj.astype(jnp.float32).reshape(RESP, KVH, group_size, HD)
    key_heads = key_proj.astype(jnp.float32).reshape(RESP, KVH, HD)
    value_heads = value_proj.astype(jnp.float32).reshape(RESP, KVH, HD)
    scores = jnp.einsum('qkgd,pkd->kgqp', query_heads, key_heads) * score_scale
    positions = jnp.arange(RESP)
    allowed = (positions[None, :] <= positions[:, None]) & (positions[None, :] < length)
    scores = jnp.where(allowed[None, None], scores, -1e+30)
    top_score = lax.optimization_barrier(jnp.max(scores, axis=-1, keepdims=True))
    weights = jnp.exp(scores - top_score)
    pre_probs = (weights / lax.optimization_barrier(jnp.sum(weights, axis=-1, keepdims=True))).astype(jnp.bfloat16)
    attended = jnp.einsum('kgqp,pkd->qkgd', pre_probs.astype(jnp.float32), value_heads)
    attended = attended.astype(jnp.bfloat16).reshape(RESP, QH * HD)
    group_cols = QH * HD // N_TP
    pieces = attended.astype(jnp.float32).reshape(RESP, N_TP, group_cols)
    blocks = w_out.astype(jnp.float32).reshape(N_TP, group_cols, D)
    partials = jnp.einsum('qgc,gcd->gqd', pieces, blocks)
    rounded = lax.optimization_barrier(partials.astype(jnp.bfloat16))
    output = lax.optimization_barrier(jnp.sum(rounded.astype(jnp.float32), axis=0))
    row_valid = positions < length
    return jnp.where(row_valid[:, None], output, 0.0)

def reference(dest_slot, finished, lengths, cache_keys, cache_values, responses, dec_queries, new_keys, new_values, norm_gain, w_query, w_key, w_value, w_out):
    inverse = jnp.zeros((SLOTS,), jnp.int32).at[dest_slot].set(jnp.arange(SLOTS, dtype=jnp.int32))
    slot_keys = cache_keys[inverse]
    slot_values = cache_values[inverse]
    slot_states = responses[inverse]
    slot_length = lengths[inverse]
    slot_done = finished[inverse]

    def decode_entry(packed):
        return decode_slot(*packed)
    decoded = lax.map(decode_entry, (dec_queries, new_keys, new_values, slot_keys, slot_values, slot_length))
    decode_out = jnp.where(slot_done[:, None, None] == 0, decoded, jnp.zeros_like(decoded))

    def prefill_entry(packed):
        return prefill_slot(packed[0], packed[1], norm_gain, w_query, w_key, w_value, w_out)
    filled = lax.map(prefill_entry, (slot_states, slot_length))
    prefill_out = jnp.where(slot_done[:, None, None] == 1, filled, 0.0).astype(jnp.bfloat16)
    return (decode_out, prefill_out)
```

```python
import math

import jax
import jax.numpy as jnp
from jax import lax
from jax.experimental import pallas as pl
from jax.experimental.pallas import tpu as pltpu
from jax.sharding import PartitionSpec as P

QH = 32
KVH = 8
HD = 128
PROMPT = 128


BLOCK = 64
NEG = -1e30
CAPACITIES = (320, 448, 512, 576, 640, 704, 768)
FIRST_NEAR = 256
FIRST_FAR = 192


def attend_kernel(base, start_ref, query_ref, keyval_ref, out_ref):
    first_row = pl.program_id(0) * BLOCK
    window = keyval_ref[pl.ds(pl.multiple_of(first_row, BLOCK), BLOCK + PROMPT), :]
    half = window.shape[1] // 2
    group_size = QH // KVH
    shape = (BLOCK, BLOCK + PROMPT)
    query_pos = base + first_row + lax.broadcasted_iota(jnp.int32, shape, 0)
    key_pos = base + first_row - PROMPT + lax.broadcasted_iota(jnp.int32, shape, 1)
    allowed = (key_pos >= start_ref[...]) & (key_pos <= query_pos)
    bias = jnp.where(allowed, 0.0, NEG)
    bias = jnp.concatenate([bias] * group_size, axis=0)
    for head in range(half // HD):
        columns = [(head * group_size + g) * HD for g in range(group_size)]
        queries = jnp.concatenate([query_ref[:, c : c + HD] for c in columns], axis=0)
        keys = window[:, head * HD : (head + 1) * HD]
        values = window[:, half + head * HD : half + (head + 1) * HD]
        scores = lax.dot_general(
            queries, keys, (((1,), (1,)), ((), ())), preferred_element_type=jnp.float32
        )
        scores = scores * (1.0 / math.sqrt(HD)) + bias
        weights = jnp.exp(scores - jnp.max(scores, axis=-1, keepdims=True))
        probs = (weights / jnp.sum(weights, axis=-1, keepdims=True)).astype(jnp.bfloat16)
        mixed = jnp.dot(probs, values, preferred_element_type=jnp.float32).astype(jnp.bfloat16)
        for g, c in enumerate(columns):
            out_ref[:, c : c + HD] = mixed[g * BLOCK : (g + 1) * BLOCK]


def attend(qkv, earlier, row_start, base):
    tokens = qkv.shape[0]
    kv_width = earlier.shape[1]
    q_width = qkv.shape[1] - kv_width
    keyval = jnp.concatenate([earlier, qkv[:, q_width:]], axis=0)
    out = pl.pallas_call(
        lambda *refs: attend_kernel(base, *refs),
        grid=(tokens // BLOCK,),
        in_specs=[
            pl.BlockSpec((BLOCK, 1), lambda b: (b, 0)),
            pl.BlockSpec((BLOCK, q_width), lambda b: (b, 0)),
            pl.BlockSpec((tokens + PROMPT, kv_width), lambda b: (0, 0)),
        ],
        out_specs=pl.BlockSpec((BLOCK, q_width), lambda b: (b, 0)),
        out_shape=jax.ShapeDtypeStruct((tokens, q_width), jnp.bfloat16),
        compiler_params=pltpu.CompilerParams(vmem_limit_bytes=16 * 2**20),
        cost_estimate=pl.CostEstimate(
            flops=4 * tokens * (BLOCK + PROMPT) * q_width,
            bytes_accessed=2 * tokens * (2 * q_width + kv_width),
            transcendentals=tokens * (BLOCK + PROMPT) * (q_width // HD),
        ),
        name="prefill_attention",
    )(row_start, qkv, keyval)
    return out, keyval[tokens:]


def decode_kernel(length_ref, active_ref, query_ref, new_key_ref, new_value_ref, key_ref, value_ref, out_ref):
    row = pl.program_id(0)

    @pl.when(active_ref[row] == 0)
    def _():
        out_ref[...] = jnp.zeros_like(out_ref)

    @pl.when(active_ref[row] != 0)
    def _():
        scale = 1.0 / math.sqrt(HD)
        valid = PROMPT + length_ref[row]
        keys, values = key_ref[0], value_ref[0]
        nums = (((1,), (1,)), ((), ()))
        for head in range(query_ref.shape[1]):
            queries = query_ref[0, head]
            lanes = slice(head * HD, (head + 1) * HD)
            old = lax.dot_general(queries, keys[:, lanes], nums, preferred_element_type=jnp.float32)
            new = lax.dot_general(
                queries, new_key_ref[0, head], nums, preferred_element_type=jnp.float32
            )
            position = lax.broadcasted_iota(jnp.int32, old.shape, 1)
            old = jnp.where(position < valid, old * scale, NEG)
            step = lax.broadcasted_iota(jnp.int32, new.shape, 0) // (QH // KVH)
            new = jnp.where(lax.broadcasted_iota(jnp.int32, new.shape, 1) <= step, new * scale, NEG)
            top = jnp.maximum(
                jnp.max(old, axis=-1, keepdims=True), jnp.max(new, axis=-1, keepdims=True)
            )
            old_weights, new_weights = jnp.exp(old - top), jnp.exp(new - top)
            total = jnp.sum(old_weights, axis=-1, keepdims=True) + jnp.sum(
                new_weights, axis=-1, keepdims=True
            )
            mixed = jnp.dot(
                (old_weights / total).astype(jnp.bfloat16),
                values[:, lanes],
                preferred_element_type=jnp.float32,
            ) + jnp.dot(
                (new_weights / total).astype(jnp.bfloat16),
                new_value_ref[0, head],
                preferred_element_type=jnp.float32,
            )
            out_ref[0, head] = mixed.astype(jnp.bfloat16)


def decode_here(length, active, fresh, cache_keys, cache_values, steps):
    rows, cache_len, kv_width = cache_keys.shape
    heads = kv_width // HD
    group = QH // KVH
    q_width = heads * group * HD
    fresh = fresh.reshape(rows, steps, q_width + 2 * kv_width)
    queries = fresh[:, :, :q_width].reshape(rows, steps, heads, group, HD)
    queries = queries.transpose(0, 2, 1, 3, 4).reshape(rows, heads, steps * group, HD)
    new = fresh[:, :, q_width:].reshape(rows, steps, 2, heads, HD).transpose(2, 0, 3, 1, 4)
    new = jnp.pad(new, ((0, 0), (0, 0), (0, 0), (0, 16 - steps), (0, 0)))
    small = lambda n: pl.BlockSpec((1, heads, n, HD), lambda r, *_: (r, 0, 0, 0))
    cache = pl.BlockSpec((1, cache_len, kv_width), lambda r, *_: (r, 0, 0))
    out = pl.pallas_call(
        decode_kernel,
        grid_spec=pltpu.PrefetchScalarGridSpec(
            num_scalar_prefetch=2,
            grid=(rows,),
            in_specs=[small(steps * group), small(16), small(16), cache, cache],
            out_specs=small(steps * group),
        ),
        out_shape=jax.ShapeDtypeStruct((rows, heads, steps * group, HD), jnp.bfloat16),
        compiler_params=pltpu.CompilerParams(vmem_limit_bytes=16 * 2**20),
        cost_estimate=pl.CostEstimate(
            flops=4 * rows * cache_len * steps * q_width,
            bytes_accessed=8 * rows * cache_len * kv_width,
            transcendentals=0,
        ),
        name="decode_attention",
    )(length, active, queries, new[0], new[1], cache_keys, cache_values)
    out = out.reshape(rows, heads, steps, group, HD).transpose(0, 2, 1, 3, 4)
    return out.reshape(rows, steps * q_width)


def pick(mask, values):
    return jnp.dot(
        mask.astype(jnp.bfloat16), values, preferred_element_type=jnp.float32
    ).astype(jnp.bfloat16)


def two_shift_body(
    dest_slot,
    finished,
    lengths,
    cache_keys,
    cache_values,
    responses,
    dec_queries,
    new_keys,
    new_values,
    norm_gain,
    w_query,
    w_key,
    w_value,
    w_out,
):
    count = lax.axis_size("inst")
    here = lax.axis_index("inst")
    part = lax.axis_index("tp")
    tp = lax.axis_size("tp")
    reps = lax.axis_size("rep")
    rows, resp_len, width = responses.shape
    steps = dec_queries.shape[1]
    near, far = 1, count // 2
    cap = rows // 2
    full_cap = cap * resp_len

    def along(value, shift):
        return lax.ppermute(value, "inst", [(i, (i + shift) % count) for i in range(count)])

    def across(value):
        return lax.ppermute(value, "tp", [(i, i ^ 2) for i in range(tp)])

    def beside(value):
        return lax.ppermute(value, "tp", [(i, i ^ 1) for i in range(tp)])

    slots = dest_slot.reshape(count, rows)
    shift = (slots // rows - jnp.arange(count)[:, None]) % count
    earlier = jnp.arange(rows)[None, :] < jnp.arange(rows)[:, None]

    def at(table, shift_back):
        return lax.dynamic_index_in_dim(table, (here - shift_back) % count, 0, keepdims=False)

    def rank_of(own_shift):
        same = own_shift[:, None] == own_shift[None, :]
        return jnp.sum((same & earlier).astype(jnp.int32), axis=1)

    own_slots, own_shift = at(slots, 0), at(shift, 0)
    own_rank = rank_of(own_shift)

    def layout(length, done, row_shift, which):
        used = jnp.where((row_shift == which) & (done == 1), length, 0)
        offset = jnp.sum(jnp.where(earlier, used[None, :], 0), axis=1)
        return used, offset, jnp.sum(used)

    def places(used, offset):
        inside = jnp.arange(resp_len)[None, :] < used[:, None]
        return jnp.where(inside, offset[:, None] + jnp.arange(resp_len)[None, :], -1)

    def starts(used, offset):
        token = jnp.arange(full_cap, dtype=jnp.int32)
        begun = (offset[None, :] <= token[:, None]) & (used[None, :] > 0)
        return jnp.max(jnp.where(begun, offset[None, :], 0), axis=1)[:, None]

    used_near, offset_near, total_near = layout(lengths, finished, own_shift, near)
    used_far, offset_far, total_far = layout(lengths, finished, own_shift, far)
    place_near = places(used_near, offset_near).reshape(1, rows * resp_len)
    place_far = places(used_far, offset_far).reshape(1, rows * resp_len)
    flat = responses.reshape(rows * resp_len, width)

    def packed(place, low, high):
        token = jnp.arange(low, high, dtype=jnp.int32)[:, None]
        return pick(token == place, flat)

    most = jnp.maximum(total_near, total_far)
    meta = jnp.concatenate([lengths + 1024 * finished, most[None]])
    from_near, from_far = along(meta, near), along(meta, far)
    others = [along(meta, k) for k in range(1, count) if k not in (near, far)]
    for other in [from_near, from_far] + others:
        most = jnp.maximum(most, other[rows])
    for k in range(1, reps):
        most = jnp.maximum(
            most, lax.ppermute(most, "rep", [(i, (i + k) % reps) for i in range(reps)])
        )

    fresh = jnp.concatenate([dec_queries, new_keys, new_values], axis=2)
    fresh = fresh.reshape(rows, -1)

    def slot_of(shift_back, row_rank, row_shift, which):
        source_slots = at(slots, shift_back)
        source_shift = at(shift, shift_back)
        local = jnp.where(source_shift == which, source_slots - here * rows, -1)
        hit = local[None, :] == jnp.arange(rows)[:, None]
        return hit

    def rank_mask(row_shift, row_rank, which):
        member = (row_shift == which)[:, None]
        return member & (row_rank[:, None] == jnp.arange(cap)[None, :])

    near_shift, far_shift = at(shift, near), at(shift, far)
    near_rank, far_rank = rank_of(near_shift), rank_of(far_shift)
    near_hit = slot_of(near, near_rank, near_shift, near)
    far_hit = slot_of(far, far_rank, far_shift, far)
    near_slot = jnp.any(near_hit[:, :, None] & rank_mask(near_shift, near_rank, near)[None], axis=1)
    far_slot = jnp.any(far_hit[:, :, None] & rank_mask(far_shift, far_rank, far)[None], axis=1)
    back_near = along(pick(near_slot.T, fresh), -near)
    back_far = along(pick(far_slot.T, fresh), -far)
    own_near = rank_mask(own_shift, own_rank, near)
    own_far = rank_mask(own_shift, own_rank, far)
    own_group = jnp.concatenate([own_near, own_far], axis=1)
    own_fresh = pick(own_group, jnp.concatenate([back_near, back_far], axis=0))
    decoded = decode_here(lengths, 1 - finished, own_fresh, cache_keys, cache_values, steps)
    came_near = along(pick(own_near.T, decoded), near)
    came_far = along(pick(own_far.T, decoded), far)

    order = [part, part ^ 2, part ^ 1, part ^ 3]
    weights = jnp.concatenate([w_query, w_key, w_value], axis=1)
    gained = (weights.astype(jnp.float32) * norm_gain[:, None]).astype(jnp.bfloat16)
    w_qkv = jnp.concatenate(
        [lax.dynamic_slice_in_dim(gained, b * width, width, 0) for b in order], axis=0
    )
    w_blocks = [lax.dynamic_slice_in_dim(w_out, b * width, width, 1) for b in order]
    w_keep = jnp.concatenate(w_blocks[:2], axis=1)
    w_send = jnp.concatenate(w_blocks[2:], axis=1)

    def gather(own):
        chip = jnp.concatenate([own, across(own)], axis=1)
        return jnp.concatenate([chip, beside(chip)], axis=1)

    def project(states):
        states_f = states.astype(jnp.float32)
        inverse = lax.rsqrt(jnp.mean(states_f * states_f, axis=1, keepdims=True) + 1e-06)
        return (jnp.dot(states, w_qkv, preferred_element_type=jnp.float32) * inverse).astype(
            jnp.bfloat16
        )

    def reduce(attended):
        send = jnp.dot(attended, w_send, preferred_element_type=jnp.float32).astype(jnp.bfloat16)
        came = beside(send)
        chip = jnp.dot(attended, w_keep, preferred_element_type=jnp.float32) + came.astype(
            jnp.float32
        )
        other = across(chip[:, width:].astype(jnp.bfloat16))
        return (chip[:, :width] + other.astype(jnp.float32)).astype(jnp.bfloat16)

    start_near = starts(used_near, offset_near)

    near_states0 = packed(place_near, 0, FIRST_NEAR)
    far_states0 = packed(place_far, 0, FIRST_FAR)
    far_came0 = along(far_states0, far)
    near_gathered0 = gather(near_states0)
    near_qkv0 = project(near_gathered0)

    def arrived(meta_came, row_shift, which):
        return layout(meta_came[:rows] % 1024, meta_came[:rows] // 1024, row_shift, which)

    used_a, offset_a, _ = arrived(from_near, near_shift, near)
    used_b, offset_b, _ = arrived(from_far, far_shift, far)
    start_far = starts(used_b, offset_b)

    def slot_places(hit, used, offset):
        table = places(used, offset)
        return jnp.max(jnp.where(hit[:, :, None], table[None], -1), axis=1).reshape(-1, 1)

    slot_near = slot_places(near_hit, used_a, offset_a)
    slot_far = slot_places(far_hit, used_b, offset_b)
    kv_width = w_key.shape[1] + w_value.shape[1]

    def rest(capacity):
        def run():
            none = jnp.zeros((PROMPT, kv_width), jnp.bfloat16)
            far_cuts = [FIRST_FAR, FIRST_FAR + (capacity - FIRST_FAR) // (2 * BLOCK) * BLOCK, capacity]
            far_cuts = sorted(set(far_cuts))
            near_cuts = sorted(set([FIRST_NEAR, capacity]))
            far_states = [far_came0] + [
                along(packed(place_far, a, b), far) for a, b in zip(far_cuts, far_cuts[1:])
            ]
            qkv = [near_qkv0] + [
                project(gather(packed(place_near, a, b))) for a, b in zip(near_cuts, near_cuts[1:])
            ]
            results = []
            tail = none
            low = 0
            for chunk in qkv:
                high = low + chunk.shape[0]
                attended, tail = attend(chunk, tail, start_near[low:high], low)
                results.append(along(reduce(attended), near))
                low = high
            token = jnp.arange(capacity, dtype=jnp.int32)[None, :]
            from_a = pick(slot_near == token, jnp.concatenate(results, axis=0))
            results = []
            tail = none
            low = 0
            for states in far_states:
                high = low + states.shape[0]
                attended, tail = attend(project(gather(states)), tail, start_far[low:high], low)
                results.append(reduce(attended))
                low = high
            from_b = jnp.dot(
                (slot_far == token).astype(jnp.bfloat16),
                jnp.concatenate(results, axis=0),
                preferred_element_type=jnp.float32,
            )
            return (from_b + from_a.astype(jnp.float32)).astype(jnp.bfloat16)

        return run

    capacities = [c for c in CAPACITIES if c < full_cap] + [full_cap]
    branch = jnp.sum(jnp.array([most > c for c in capacities[:-1]], jnp.int32))
    prefilled = lax.switch(branch, [rest(c) for c in capacities])
    active_slot = jnp.concatenate([near_slot, far_slot], axis=1)
    decoded = pick(active_slot, jnp.concatenate([came_near, came_far], axis=0))
    return (
        decoded.reshape(rows, steps, -1),
        prefilled.reshape(rows, resp_len, width),
    )


def place_rows(values, index, count):
    buffer = jnp.zeros((count,) + values.shape[1:], values.dtype)
    return buffer.at[index].set(values)


def decode_rows(queries, fresh_keys, fresh_values, old_keys, old_values, length):
    row_count, step_count, width = queries.shape
    heads_kv = old_keys.shape[2] // HD
    group_size = QH // KVH
    cache_len = old_keys.shape[1]
    score_scale = 1.0 / math.sqrt(HD)
    query_heads = queries.reshape(row_count, step_count, heads_kv, group_size, HD)
    key_heads = old_keys.reshape(row_count, cache_len, heads_kv, HD)
    value_heads = old_values.reshape(row_count, cache_len, heads_kv, HD)
    fresh_key_heads = fresh_keys.reshape(row_count, step_count, heads_kv, HD)
    fresh_value_heads = fresh_values.reshape(row_count, step_count, heads_kv, HD)
    old_scores = (
        jnp.einsum("rskgd,rpkd->rskgp", query_heads, key_heads, preferred_element_type=jnp.float32)
        * score_scale
    )
    new_scores = (
        jnp.einsum(
            "rskgd,rtkd->rskgt", query_heads, fresh_key_heads, preferred_element_type=jnp.float32
        )
        * score_scale
    )
    old_valid = jnp.arange(cache_len)[None, :] < PROMPT + length[:, None]
    step_index = jnp.arange(step_count)
    new_valid = step_index[None, :] <= step_index[:, None]
    old_scores = jnp.where(old_valid[:, None, None, None, :], old_scores, -1e30)
    new_scores = jnp.where(new_valid[None, :, None, None, :], new_scores, -1e30)
    top_score = jnp.maximum(
        jnp.max(old_scores, axis=-1, keepdims=True), jnp.max(new_scores, axis=-1, keepdims=True)
    )
    old_weights = jnp.exp(old_scores - top_score)
    new_weights = jnp.exp(new_scores - top_score)
    totals = jnp.sum(old_weights, axis=-1, keepdims=True) + jnp.sum(
        new_weights, axis=-1, keepdims=True
    )
    old_probs = (old_weights / totals).astype(jnp.bfloat16)
    new_probs = (new_weights / totals).astype(jnp.bfloat16)
    mixed = jnp.einsum(
        "rskgp,rpkd->rskgd", old_probs, value_heads, preferred_element_type=jnp.float32
    )
    mixed = mixed + jnp.einsum(
        "rskgt,rtkd->rskgd", new_probs, fresh_value_heads, preferred_element_type=jnp.float32
    )
    return mixed.astype(jnp.bfloat16).reshape(row_count, step_count, width)


def prefill_rows(states, length, norm_gain, w_query, w_key, w_value, w_out):
    row_count, resp_len, width = states.shape
    heads_kv = w_key.shape[1] // HD
    group_size = QH // KVH
    score_scale = 1.0 / math.sqrt(HD)
    states_f = states.astype(jnp.float32)
    mean_square = jnp.mean(states_f * states_f, axis=-1, keepdims=True)
    normed = (states_f * lax.rsqrt(mean_square + 1e-06) * norm_gain).astype(jnp.bfloat16)
    flat_rows = normed.reshape(row_count * resp_len, width)
    query_proj = jnp.dot(flat_rows, w_query, preferred_element_type=jnp.float32).astype(
        jnp.bfloat16
    )
    key_proj = jnp.dot(flat_rows, w_key, preferred_element_type=jnp.float32).astype(jnp.bfloat16)
    value_proj = jnp.dot(flat_rows, w_value, preferred_element_type=jnp.float32).astype(
        jnp.bfloat16
    )
    query_heads = query_proj.reshape(row_count, resp_len, heads_kv, group_size, HD)
    key_heads = key_proj.reshape(row_count, resp_len, heads_kv, HD)
    value_heads = value_proj.reshape(row_count, resp_len, heads_kv, HD)
    scores = (
        jnp.einsum("rqkgd,rpkd->rkgqp", query_heads, key_heads, preferred_element_type=jnp.float32)
        * score_scale
    )
    positions = jnp.arange(resp_len)
    causal = positions[None, :] <= positions[:, None]
    allowed = causal[None, :, :] & (positions[None, None, :] < length[:, None, None])
    scores = jnp.where(allowed[:, None, None], scores, -1e30)
    top_score = jnp.max(scores, axis=-1, keepdims=True)
    weights = jnp.exp(scores - top_score)
    pre_probs = (weights / jnp.sum(weights, axis=-1, keepdims=True)).astype(jnp.bfloat16)
    attended = jnp.einsum(
        "rkgqp,rpkd->rqkgd", pre_probs, value_heads, preferred_element_type=jnp.float32
    )
    attended = attended.astype(jnp.bfloat16).reshape(
        row_count * resp_len, heads_kv * group_size * HD
    )
    return jnp.dot(attended, w_out, preferred_element_type=jnp.float32)


def general_body(
    dest_slot,
    finished,
    lengths,
    cache_keys,
    cache_values,
    responses,
    dec_queries,
    new_keys,
    new_values,
    norm_gain,
    w_query,
    w_key,
    w_value,
    w_out,
):
    inst_count = lax.axis_size("inst")
    here_index = lax.axis_index("inst")
    row_count = finished.shape[0]
    slot_count = dest_slot.shape[0]
    per_target = max(2, 2 * row_count // inst_count)
    bucket_count = inst_count * per_target
    target = (dest_slot // row_count).reshape(inst_count, row_count)
    earlier = jnp.arange(row_count)[None, :] < jnp.arange(row_count)[:, None]
    same_target = target[:, :, None] == target[:, None, :]
    order_rank = jnp.sum(jnp.where(same_target & earlier[None], 1, 0), axis=2).astype(jnp.int32)
    bucket = (target * per_target + order_rank).reshape(slot_count)
    own_bucket = lax.dynamic_slice_in_dim(bucket, here_index * row_count, row_count)
    source = (
        jnp.zeros((slot_count,), jnp.int32)
        .at[dest_slot]
        .set(jnp.arange(slot_count, dtype=jnp.int32))
    )
    arrivals = lax.dynamic_slice_in_dim(source, here_index * row_count, row_count)
    incoming = arrivals // row_count * per_target + order_rank.reshape(slot_count)[arrivals]
    received = (
        lax.all_to_all(
            place_rows(responses, own_bucket, bucket_count),
            "inst",
            split_axis=0,
            concat_axis=0,
            tiled=True,
        ),
        lax.all_to_all(
            place_rows(finished, own_bucket, bucket_count),
            "inst",
            split_axis=0,
            concat_axis=0,
            tiled=True,
        ),
        lax.all_to_all(
            place_rows(lengths, own_bucket, bucket_count),
            "inst",
            split_axis=0,
            concat_axis=0,
            tiled=True,
        ),
    )
    slot_states = received[0][incoming]
    slot_done = received[1][incoming]
    slot_length = received[2][incoming]
    moved_caches = (
        lax.all_to_all(
            place_rows(cache_keys, own_bucket, bucket_count),
            "inst",
            split_axis=0,
            concat_axis=0,
            tiled=True,
        ),
        lax.all_to_all(
            place_rows(cache_values, own_bucket, bucket_count),
            "inst",
            split_axis=0,
            concat_axis=0,
            tiled=True,
        ),
    )
    decoded = decode_rows(
        dec_queries,
        new_keys,
        new_values,
        moved_caches[0][incoming],
        moved_caches[1][incoming],
        slot_length,
    )
    decoded = jnp.where(slot_done[:, None, None] == 0, decoded, jnp.zeros_like(decoded))
    states = lax.all_gather(slot_states, "tp", axis=2, tiled=True)
    partial_value = prefill_rows(states, slot_length, norm_gain, w_query, w_key, w_value, w_out)
    summed = lax.psum_scatter(
        partial_value.astype(jnp.bfloat16), "tp", scatter_dimension=1, tiled=True
    ).astype(jnp.float32)
    resp_len = states.shape[1]
    summed = summed.reshape(row_count, resp_len, -1)
    keep_mask = (jnp.arange(resp_len)[None, :] < slot_length[:, None]) & (slot_done[:, None] == 1)
    prefilled = jnp.where(keep_mask[:, :, None], summed, 0.0).astype(jnp.bfloat16)
    return (decoded, prefilled)


def body(*args):
    row_count = args[1].shape[0]
    inst_count = lax.axis_size("inst")
    two_groups = 2 * (2 * row_count // inst_count) == row_count and inst_count > 2
    if two_groups and lax.axis_size("tp") == 4:
        return two_shift_body(*args)
    return general_body(*args)


def solution(mesh):
    return jax.shard_map(
        body,
        mesh=mesh,
        in_specs=(
            P("rep"),
            P(("rep", "inst")),
            P(("rep", "inst")),
            P(("rep", "inst"), None, "tp"),
            P(("rep", "inst"), None, "tp"),
            P(("rep", "inst"), None, "tp"),
            P(("rep", "inst"), None, "tp"),
            P(("rep", "inst"), None, "tp"),
            P(("rep", "inst"), None, "tp"),
            P(),
            P(None, "tp"),
            P(None, "tp"),
            P(None, "tp"),
            P("tp", None),
        ),
        out_specs=(P(("rep", "inst"), None, "tp"), P(("rep", "inst"), None, "tp")),
        check_vma=False,
    )
```

```python
import math

import jax
import jax.numpy as jnp
from jax import lax
from jax.experimental import pallas as pl
from jax.experimental.pallas import tpu as pltpu
from jax.sharding import PartitionSpec as P

QH = 32
KVH = 8
HD = 128
PROMPT = 128


BLOCK = 64
TILE = 512
COST = 3
NEAR_SHARES = (320, 384)
FAR_SHARES = (256, 256, 192)
NEG = -1e30
CAPACITY = 704


def layer_kernel(
    base,
    part_ref,
    start_ref,
    own_ref,
    across_ref,
    beside_ref,
    earlier_ref,
    gain_ref,
    wq_ref,
    wk_ref,
    wv_ref,
    w_out,
    send_ref,
    keep_ref,
    later_ref,
    states,
    inverse,
    qkv,
    attended,
):
    tokens, width = own_ref.shape
    features = states.shape[1]
    q_width = w_out.shape[0]
    kv_width = wk_ref.shape[1]
    group_size = QH // KVH
    part = part_ref[0]

    def columns_of(block):
        return pl.ds(pl.multiple_of(block * width, 128), width)

    states[:, columns_of(part)] = own_ref[...]
    states[:, columns_of(part ^ 2)] = across_ref[...]
    states[:, columns_of(part ^ 1)] = beside_ref[:, :width]
    states[:, columns_of(part ^ 3)] = beside_ref[:, width:]
    qkv[:PROMPT, q_width:] = earlier_ref[...]

    def norm_rows(b, carry):
        rows = pl.ds(pl.multiple_of(b * BLOCK, BLOCK), BLOCK)
        total = jnp.zeros((BLOCK, 128), jnp.float32)
        for c in range(0, features, 128):
            value = states[rows, c : c + 128].astype(jnp.float32) * gain_ref[:, c : c + 128]
            total = total + value * value
        mean = jnp.sum(total, axis=1, keepdims=True) * (1.0 / features)
        inverse[rows, :] = jnp.broadcast_to(lax.rsqrt(mean + 1e-06), (BLOCK, 128))
        return carry

    lax.fori_loop(0, tokens // BLOCK, norm_rows, 0)
    def project(t, carry):
        columns = pl.ds(pl.multiple_of(t * TILE, TILE), TILE)
        product = jnp.dot(states[...], wq_ref[:, columns], preferred_element_type=jnp.float32)
        scale = inverse[...] * (math.log2(math.e) / math.sqrt(HD))
        scale = jnp.concatenate([scale] * (TILE // 128), axis=1)
        qkv[PROMPT:, columns] = (product * scale).astype(jnp.bfloat16)
        return carry

    lax.fori_loop(0, q_width // TILE, project, 0)
    scale = jnp.concatenate([inverse[...]] * (kv_width // 128), axis=1)
    for first, w_ref in ((q_width, wk_ref), (q_width + kv_width, wv_ref)):
        product = jnp.dot(states[...], w_ref[...], preferred_element_type=jnp.float32)
        qkv[PROMPT:, first : first + kv_width] = (product * scale).astype(jnp.bfloat16)

    shape = (BLOCK, BLOCK + PROMPT)

    def attend(b, carry):
        row = pl.multiple_of(b * BLOCK, BLOCK)
        query_pos = base + row + lax.broadcasted_iota(jnp.int32, shape, 0)
        key_pos = base + row - PROMPT + lax.broadcasted_iota(jnp.int32, shape, 1)
        allowed = (key_pos >= start_ref[pl.ds(row, BLOCK), :]) & (key_pos <= query_pos)
        bias = jnp.where(allowed, 0.0, NEG)
        bias = jnp.concatenate([bias] * group_size, axis=0)
        query_rows = pl.ds(pl.multiple_of(row + PROMPT, BLOCK), BLOCK)
        key_rows = pl.ds(row, BLOCK + PROMPT)
        for head in range(kv_width // HD):
            columns = [(head * group_size + g) * HD for g in range(group_size)]
            queries = jnp.concatenate([qkv[query_rows, c : c + HD] for c in columns], axis=0)
            first = q_width + head * HD
            keys = qkv[key_rows, first : first + HD]
            values = qkv[key_rows, first + kv_width : first + kv_width + HD]
            scores = lax.dot_general(
                queries, keys, (((1,), (1,)), ((), ())), preferred_element_type=jnp.float32
            )
            scores = scores + bias
            weights = jnp.exp2(scores - jnp.max(scores, axis=-1, keepdims=True))
            values = jnp.concatenate([values, jnp.ones_like(values)], axis=1)
            mixed = jnp.dot(
                weights.astype(jnp.bfloat16), values, preferred_element_type=jnp.float32
            )
            mixed = (mixed[:, :HD] * (1.0 / mixed[:, HD:])).astype(jnp.bfloat16)
            for g, c in enumerate(columns):
                attended[pl.ds(row, BLOCK), c : c + HD] = mixed[g * BLOCK : (g + 1) * BLOCK]
        return carry

    lax.fori_loop(0, tokens // BLOCK, attend, 0)
    later_ref[...] = qkv[tokens:, q_width:]

    def out_block(place, carry):
        block = part ^ jnp.where(place == 0, 1, jnp.where(place == 1, 3, jnp.where(place == 2, 0, 2)))
        product = jnp.dot(
            attended[...], w_out[:, columns_of(block)], preferred_element_type=jnp.float32
        ).astype(jnp.bfloat16)

        @pl.when(place < 2)
        def _():
            send_ref[:, columns_of(place)] = product

        @pl.when(place >= 2)
        def _():
            keep_ref[:, columns_of(place - 2)] = product

        return carry

    lax.fori_loop(0, 4, out_block, 0)


def layer(base, part, row_start, own, other, beside, earlier, inverse_gain, weights):
    tokens, width = own.shape
    w_out = weights[3]
    q_width, features = w_out.shape
    kv_width = weights[1].shape[1]
    whole = pl.BlockSpec(memory_space=pltpu.VMEM)
    half = jax.ShapeDtypeStruct((tokens, 2 * width), jnp.bfloat16)
    return pl.pallas_call(
        lambda *refs: layer_kernel(base, *refs),
        in_specs=[pl.BlockSpec(memory_space=pltpu.SMEM)] + [whole] * 10,
        out_specs=[whole] * 3,
        out_shape=[half, half, jax.ShapeDtypeStruct((PROMPT, 2 * kv_width), jnp.bfloat16)],
        scratch_shapes=[
            pltpu.VMEM((tokens, features), jnp.bfloat16),
            pltpu.VMEM((tokens, 128), jnp.float32),
            pltpu.VMEM((tokens + PROMPT, q_width + 2 * kv_width), jnp.bfloat16),
            pltpu.VMEM((tokens, q_width), jnp.bfloat16),
        ],
        compiler_params=pltpu.CompilerParams(vmem_limit_bytes=28 * 2**20),
        cost_estimate=pl.CostEstimate(
            flops=COST * 2 * tokens * features * (2 * q_width + 2 * kv_width),
            bytes_accessed=1024,
            transcendentals=0,
        ),
        name="prefill_layer",
    )(part[None], row_start, own, other, beside, earlier, inverse_gain, *weights)


def unpack_kernel(cuts, used_ref, offset_ref, *refs):
    pieces, out_ref, held = refs[:-2], refs[-2], refs[-1]
    step = pl.program_id(0)

    @pl.when(step == 0)
    def _():
        for low, piece in zip(cuts, pieces):
            held[low : low + piece.shape[0], :] = piece[...]
        end = cuts[-1] + pieces[-1].shape[0]
        held[end:, :] = jnp.zeros((held.shape[0] - end, held.shape[1]), held.dtype)

    per_step, resp_len = out_ref.shape[:2]
    token = lax.broadcasted_iota(jnp.int32, (resp_len, 2 * resp_len), 0)
    place = lax.broadcasted_iota(jnp.int32, (resp_len, 2 * resp_len), 1)
    for k in range(per_step):
        offset = offset_ref[step * per_step + k]
        first = pl.multiple_of(offset // 16 * 16, 16)
        window = held[pl.ds(first, 2 * resp_len), :]
        mask = (place == token + (offset - first)) & (token < used_ref[step * per_step + k])
        mask = jnp.where(mask, 1.0, 0.0).astype(jnp.bfloat16)
        out_ref[k] = jnp.dot(mask, window, preferred_element_type=jnp.float32).astype(jnp.bfloat16)


def unpack(used, offset, pieces, cuts, resp_len):
    slots, width = used.shape[0], pieces[0].shape[1]
    per_step = 2 if slots % 2 == 0 else 1
    full = lambda piece: pl.BlockSpec(piece.shape, lambda s, *_: (0, 0))
    return pl.pallas_call(
        lambda *refs: unpack_kernel(cuts, *refs),
        grid_spec=pltpu.PrefetchScalarGridSpec(
            num_scalar_prefetch=2,
            grid=(slots // per_step,),
            in_specs=[full(piece) for piece in pieces],
            out_specs=pl.BlockSpec((per_step, resp_len, width), lambda s, *_: (s, 0, 0)),
            scratch_shapes=[pltpu.VMEM((cuts[-1] + pieces[-1].shape[0] + 2 * resp_len, width), jnp.bfloat16)],
        ),
        out_shape=jax.ShapeDtypeStruct((slots, resp_len, width), jnp.bfloat16),
        compiler_params=pltpu.CompilerParams(vmem_limit_bytes=24 * 2**20),
        name="unpack_slots",
    )(used, offset, *pieces)


def decode_kernel(length_ref, active_ref, query_ref, new_key_ref, new_value_ref, key_ref, value_ref, out_ref):
    row = pl.program_id(0)

    @pl.when(active_ref[row] == 0)
    def _():
        out_ref[...] = jnp.zeros_like(out_ref)

    @pl.when(active_ref[row] != 0)
    def _():
        scale = 1.0 / math.sqrt(HD)
        valid = PROMPT + length_ref[row]
        keys, values = key_ref[0], value_ref[0]
        nums = (((1,), (1,)), ((), ()))
        for head in range(query_ref.shape[1]):
            queries = query_ref[0, head]
            lanes = slice(head * HD, (head + 1) * HD)
            old = lax.dot_general(queries, keys[:, lanes], nums, preferred_element_type=jnp.float32)
            new = lax.dot_general(
                queries, new_key_ref[0, head], nums, preferred_element_type=jnp.float32
            )
            position = lax.broadcasted_iota(jnp.int32, old.shape, 1)
            old = jnp.where(position < valid, old * scale, NEG)
            step = lax.broadcasted_iota(jnp.int32, new.shape, 0) // (QH // KVH)
            new = jnp.where(lax.broadcasted_iota(jnp.int32, new.shape, 1) <= step, new * scale, NEG)
            top = jnp.maximum(
                jnp.max(old, axis=-1, keepdims=True), jnp.max(new, axis=-1, keepdims=True)
            )
            old_weights, new_weights = jnp.exp(old - top), jnp.exp(new - top)
            total = jnp.sum(old_weights, axis=-1, keepdims=True) + jnp.sum(
                new_weights, axis=-1, keepdims=True
            )
            mixed = jnp.dot(
                (old_weights / total).astype(jnp.bfloat16),
                values[:, lanes],
                preferred_element_type=jnp.float32,
            ) + jnp.dot(
                (new_weights / total).astype(jnp.bfloat16),
                new_value_ref[0, head],
                preferred_element_type=jnp.float32,
            )
            out_ref[0, head] = mixed.astype(jnp.bfloat16)


def decode_here(length, active, fresh, cache_keys, cache_values, steps):
    rows, cache_len, kv_width = cache_keys.shape
    heads = kv_width // HD
    group = QH // KVH
    q_width = heads * group * HD
    fresh = fresh.reshape(rows, steps, q_width + 2 * kv_width)
    queries = fresh[:, :, :q_width].reshape(rows, steps, heads, group, HD)
    queries = queries.transpose(0, 2, 1, 3, 4).reshape(rows, heads, steps * group, HD)
    new = fresh[:, :, q_width:].reshape(rows, steps, 2, heads, HD).transpose(2, 0, 3, 1, 4)
    new = jnp.pad(new, ((0, 0), (0, 0), (0, 0), (0, 16 - steps), (0, 0)))
    small = lambda n: pl.BlockSpec((1, heads, n, HD), lambda r, *_: (r, 0, 0, 0))
    cache = pl.BlockSpec((1, cache_len, kv_width), lambda r, *_: (r, 0, 0))
    out = pl.pallas_call(
        decode_kernel,
        grid_spec=pltpu.PrefetchScalarGridSpec(
            num_scalar_prefetch=2,
            grid=(rows,),
            in_specs=[small(steps * group), small(16), small(16), cache, cache],
            out_specs=small(steps * group),
        ),
        out_shape=jax.ShapeDtypeStruct((rows, heads, steps * group, HD), jnp.bfloat16),
        compiler_params=pltpu.CompilerParams(vmem_limit_bytes=16 * 2**20),
        cost_estimate=pl.CostEstimate(
            flops=4 * rows * cache_len * steps * q_width,
            bytes_accessed=8 * rows * cache_len * kv_width,
            transcendentals=0,
        ),
        name="decode_attention",
    )(length, active, queries, new[0], new[1], cache_keys, cache_values)
    out = out.reshape(rows, heads, steps, group, HD).transpose(0, 2, 1, 3, 4)
    return out.reshape(rows, steps * q_width)


def pick(mask, values):
    return jnp.dot(
        mask.astype(jnp.bfloat16), values, preferred_element_type=jnp.float32
    ).astype(jnp.bfloat16)


def two_shift_body(
    dest_slot,
    finished,
    lengths,
    cache_keys,
    cache_values,
    responses,
    dec_queries,
    new_keys,
    new_values,
    norm_gain,
    w_query,
    w_key,
    w_value,
    w_out,
):
    count = lax.axis_size("inst")
    here = lax.axis_index("inst")
    part = lax.axis_index("tp")
    tp = lax.axis_size("tp")
    reps = lax.axis_size("rep")
    rows, resp_len, width = responses.shape
    steps = dec_queries.shape[1]
    near, far = 1, count // 2
    cap = rows // 2
    full_cap = cap * resp_len

    def along(value, shift):
        return lax.ppermute(value, "inst", [(i, (i + shift) % count) for i in range(count)])

    def across(value):
        return lax.ppermute(value, "tp", [(i, i ^ 2) for i in range(tp)])

    def beside(value):
        return lax.ppermute(value, "tp", [(i, i ^ 1) for i in range(tp)])

    def ordered(value, *after):
        return lax.optimization_barrier((value,) + after)[0]

    slots = dest_slot.reshape(count, rows)
    shift = (slots // rows - jnp.arange(count)[:, None]) % count
    earlier = jnp.arange(rows)[None, :] < jnp.arange(rows)[:, None]

    def at(table, shift_back):
        return lax.dynamic_index_in_dim(table, (here - shift_back) % count, 0, keepdims=False)

    def rank_of(own_shift):
        same = own_shift[:, None] == own_shift[None, :]
        return jnp.sum((same & earlier).astype(jnp.int32), axis=1)

    own_slots, own_shift = at(slots, 0), at(shift, 0)
    own_rank = rank_of(own_shift)

    def layout(length, done, row_shift, which):
        used = jnp.where((row_shift == which) & (done == 1), length, 0)
        offset = jnp.sum(jnp.where(earlier, used[None, :], 0), axis=1)
        return used, offset, jnp.sum(used)

    def places(used, offset):
        inside = jnp.arange(resp_len)[None, :] < used[:, None]
        return jnp.where(inside, offset[:, None] + jnp.arange(resp_len)[None, :], -1)

    def starts(used, offset):
        token = jnp.arange(full_cap, dtype=jnp.int32)
        begun = (offset[None, :] <= token[:, None]) & (used[None, :] > 0)
        return jnp.max(jnp.where(begun, offset[None, :], 0), axis=1)[:, None]

    used_near, offset_near, total_near = layout(lengths, finished, own_shift, near)
    used_far, offset_far, total_far = layout(lengths, finished, own_shift, far)
    place_near = places(used_near, offset_near).reshape(1, rows * resp_len)
    place_far = places(used_far, offset_far).reshape(1, rows * resp_len)
    flat = responses.reshape(rows * resp_len, width)
    own_gain = lax.dynamic_slice_in_dim(norm_gain, part * width, width)


    def packed(place, low, high):
        token = jnp.arange(low, high, dtype=jnp.int32)[:, None]
        chosen = jnp.dot(
            (token == place).astype(jnp.bfloat16), flat, preferred_element_type=jnp.float32
        )
        return (chosen * own_gain).astype(jnp.bfloat16)

    fresh = jnp.concatenate([dec_queries, new_keys, new_values], axis=2)
    fresh = fresh.reshape(rows, -1)

    def slot_of(shift_back, row_rank, row_shift, which):
        source_slots = at(slots, shift_back)
        source_shift = at(shift, shift_back)
        local = jnp.where(source_shift == which, source_slots - here * rows, -1)
        hit = local[None, :] == jnp.arange(rows)[:, None]
        return hit

    def rank_mask(row_shift, row_rank, which):
        member = (row_shift == which)[:, None]
        return member & (row_rank[:, None] == jnp.arange(cap)[None, :])

    near_shift, far_shift = at(shift, near), at(shift, far)
    near_rank, far_rank = rank_of(near_shift), rank_of(far_shift)
    near_hit = slot_of(near, near_rank, near_shift, near)
    far_hit = slot_of(far, far_rank, far_shift, far)
    near_slot = jnp.any(near_hit[:, :, None] & rank_mask(near_shift, near_rank, near)[None], axis=1)
    far_slot = jnp.any(far_hit[:, :, None] & rank_mask(far_shift, far_rank, far)[None], axis=1)
    most = jnp.maximum(total_near, total_far)
    notes = jnp.concatenate(
        [lengths, finished, jnp.stack([most // resp_len, most % resp_len])]
    ).astype(jnp.bfloat16)

    def noted(values):
        block = jnp.pad(notes[None], ((0, 15), (0, values.shape[1] - notes.shape[0])))
        return jnp.concatenate([values, block], axis=0)

    def read(values):
        line = values[-16, : notes.shape[0]].astype(jnp.int32)
        return line[:rows], line[rows : 2 * rows], line[2 * rows] * resp_len + line[2 * rows + 1]

    own_near = rank_mask(own_shift, own_rank, near)
    own_far = rank_mask(own_shift, own_rank, far)
    away_near, away_far = noted(pick(near_slot.T, fresh)), noted(pick(far_slot.T, fresh))
    back_near, back_far = along(away_near, -near), along(away_far, -far)
    flat = ordered(flat, away_near, away_far)
    far_states = packed(place_far, 0, full_cap)
    flat = ordered(flat, far_states)
    near_states = packed(place_near, 0, full_cap)
    own_group = jnp.concatenate([own_near, own_far], axis=1)
    own_fresh = pick(own_group, jnp.concatenate([back_near[:cap], back_far[:cap]], axis=0))
    inverse_gain = (1.0 / norm_gain)[None]

    start_near = starts(used_near, offset_near)

    def arrived(meta_came, row_shift, which):
        return layout(meta_came[0], meta_came[1], row_shift, which)

    def by_slot(hit, values):
        return jnp.sum(jnp.where(hit, values[None], 0), axis=1)

    kv_width = w_key.shape[1] + w_value.shape[1]

    capacity = min(CAPACITY, full_cap)

    def cut(shares):
        marks = [0]
        for k in range(1, len(shares)):
            marks.append(round(capacity * sum(shares[:k]) / sum(shares) / BLOCK) * BLOCK)
        return marks + [capacity]

    none = jnp.zeros((PROMPT, kv_width), jnp.bfloat16)
    weights = (w_query, w_key, w_value, w_out)
    near_cuts, far_cuts = cut(NEAR_SHARES), cut(FAR_SHARES)
    near_parts = [near_states[a:b] for a, b in zip(near_cuts, near_cuts[1:])]
    near_others = [across(piece) for piece in near_parts]
    far_parts = [far_states[a:b] for a, b in zip(far_cuts, far_cuts[1:])]
    far_parts[0] = along(noted(far_parts[0]), far)
    from_far = read(far_parts[0])
    arrived_last = far_parts[0]
    far_parts[0] = far_parts[0][:-16]
    used_b, offset_b, _ = arrived(from_far, far_shift, far)
    start_far = starts(used_b, offset_b)
    lows = near_cuts[:-1] + far_cuts[:-1]
    first_far, last = len(near_parts), len(lows) - 1
    owns = near_parts + far_parts
    others, boths, cames = list(near_others), [], []
    sent, kept, crossed, chips, turned, done = [], [], [], [], [], []

    def after_kernel(value, c):
        return ordered(value, sent[c]) if 0 <= c < len(sent) else value

    def fetch(c):
        if first_far < c <= last:
            gone = owns[c - 1] if c - 1 > first_far else arrived_last
            owns[c] = along(ordered(owns[c], after_kernel(gone, c - 4)), far)

    def meet(c):
        if c == len(others):
            others.append(across(after_kernel(owns[c], c - 3)))
        other = after_kernel(others[c], c - 2)
        own = after_kernel(owns[c], c - 2)
        boths.append(jnp.concatenate([own, other], axis=1))
        cames.append(beside(boths[c]))

    def add(c):
        chips.append(after_kernel(crossed[c], c + 1))
        both = kept[c][:, width:].astype(jnp.float32) + chips[c][:, width:].astype(jnp.float32)
        both = both.astype(jnp.bfloat16)
        turned.append(across(both))
        return both

    def finish(c):
        got = after_kernel(turned[c], c + 3).astype(jnp.float32)
        both = kept[c][:, :width].astype(jnp.float32) + chips[c][:, :width].astype(jnp.float32)
        total = (both + got).astype(jnp.bfloat16)
        if c == 0:
            total = noted(total)
        done.append(along(total, near) if c < first_far else total)
        return total

    fetch(first_far + 1)
    meet(0)
    tail = none
    for c, low in enumerate(lows):
        before = [boths[0]] if c == 0 else [own_fresh] if c == 1 else []
        fetch(c + 3 if c + 3 > first_far + 1 else -1)
        if c < last:
            meet(c + 1)
            before.append(boths[c + 1])
        if c >= 2:
            before.append(add(c - 2))
        if c == 4:
            before.append(finish(0))
        if c == first_far:
            near_tail = tail
            tail = ordered(none, tail)
        tail = ordered(tail, *before)
        high = low + owns[c].shape[0]
        row_start = start_near if c < first_far else start_far
        send, keep, tail = layer(
            low,
            part,
            row_start[low:high],
            owns[c],
            others[c],
            cames[c],
            tail,
            inverse_gain,
            weights,
        )
        sent.append(send)
        kept.append(keep)
        crossed.append(beside(send))
    for c in range(len(chips), last + 1):
        gone = add(c)
    for c in range(len(done), last + 1):
        finish(c)
    decoded = decode_here(
        ordered(lengths, gone),
        1 - finished,
        own_fresh,
        cache_keys,
        cache_values,
        steps,
    )
    came_near = along(pick(own_near.T, decoded), near)
    came_far = along(pick(own_far.T, decoded), far)
    from_near, from_third = read(done[0]), read(back_near)
    for came in (from_near, from_far, from_third):
        most = jnp.maximum(most, came[2])
    most = ordered(most, gone)
    for k in range(1, reps):
        pairs = [(i, (i + k) % reps) for i in range(reps)]
        most = jnp.maximum(most, lax.ppermute(most, "rep", pairs))
    near_done, far_done = done[:first_far], done[first_far:]

    def overflow(near_x, far_x, near_kv, far_kv):
        def run(low, own, kv, row_start):
            other = across(own)
            came = beside(jnp.concatenate([own, other], axis=1))
            send, keep, _ = layer(
                low, part, row_start[low:], own, other, came, kv, inverse_gain, weights
            )
            chip = keep.astype(jnp.float32) + beside(send).astype(jnp.float32)
            got = across(chip[:, width:].astype(jnp.bfloat16))
            return (chip[:, :width] + got.astype(jnp.float32)).astype(jnp.bfloat16)

        near_more = along(run(capacity, near_x, near_kv, start_near), near)
        far_more = run(capacity, along(far_x, far), far_kv, start_far)
        return near_more, far_more

    def nothing(near_x, far_x, near_kv, far_kv):
        return jnp.zeros_like(near_x), jnp.zeros_like(far_x)

    if capacity < full_cap:
        near_more, far_more = lax.cond(
            most > capacity,
            overflow,
            nothing,
            near_states[capacity:],
            far_states[capacity:],
            near_tail,
            tail,
        )
        near_done, far_done = near_done + [near_more], far_done + [far_more]
        near_cuts, far_cuts = near_cuts + [full_cap], far_cuts + [full_cap]
    cuts = near_cuts[:-1] + [full_cap + cut_ for cut_ in far_cuts[:-1]]
    used_a, offset_a, _ = arrived(from_near, near_shift, near)
    near_used, far_used = by_slot(near_hit, used_a), by_slot(far_hit, used_b)
    near_offset, far_offset = by_slot(near_hit, offset_a), by_slot(far_hit, offset_b)
    offset = near_offset + jnp.where(far_used > 0, far_offset + full_cap, 0)
    prefilled = unpack(near_used + far_used, offset, near_done + far_done, cuts, resp_len)
    active_slot = jnp.concatenate([near_slot, far_slot], axis=1)
    decoded = pick(active_slot, jnp.concatenate([came_near, came_far], axis=0))
    return decoded.reshape(rows, steps, -1), prefilled


def place_rows(values, index, count):
    buffer = jnp.zeros((count,) + values.shape[1:], values.dtype)
    return buffer.at[index].set(values)


def decode_rows(queries, fresh_keys, fresh_values, old_keys, old_values, length):
    row_count, step_count, width = queries.shape
    heads_kv = old_keys.shape[2] // HD
    group_size = QH // KVH
    cache_len = old_keys.shape[1]
    score_scale = 1.0 / math.sqrt(HD)
    query_heads = queries.reshape(row_count, step_count, heads_kv, group_size, HD)
    key_heads = old_keys.reshape(row_count, cache_len, heads_kv, HD)
    value_heads = old_values.reshape(row_count, cache_len, heads_kv, HD)
    fresh_key_heads = fresh_keys.reshape(row_count, step_count, heads_kv, HD)
    fresh_value_heads = fresh_values.reshape(row_count, step_count, heads_kv, HD)
    old_scores = (
        jnp.einsum("rskgd,rpkd->rskgp", query_heads, key_heads, preferred_element_type=jnp.float32)
        * score_scale
    )
    new_scores = (
        jnp.einsum(
            "rskgd,rtkd->rskgt", query_heads, fresh_key_heads, preferred_element_type=jnp.float32
        )
        * score_scale
    )
    old_valid = jnp.arange(cache_len)[None, :] < PROMPT + length[:, None]
    step_index = jnp.arange(step_count)
    new_valid = step_index[None, :] <= step_index[:, None]
    old_scores = jnp.where(old_valid[:, None, None, None, :], old_scores, -1e30)
    new_scores = jnp.where(new_valid[None, :, None, None, :], new_scores, -1e30)
    top_score = jnp.maximum(
        jnp.max(old_scores, axis=-1, keepdims=True), jnp.max(new_scores, axis=-1, keepdims=True)
    )
    old_weights = jnp.exp(old_scores - top_score)
    new_weights = jnp.exp(new_scores - top_score)
    totals = jnp.sum(old_weights, axis=-1, keepdims=True) + jnp.sum(
        new_weights, axis=-1, keepdims=True
    )
    old_probs = (old_weights / totals).astype(jnp.bfloat16)
    new_probs = (new_weights / totals).astype(jnp.bfloat16)
    mixed = jnp.einsum(
        "rskgp,rpkd->rskgd", old_probs, value_heads, preferred_element_type=jnp.float32
    )
    mixed = mixed + jnp.einsum(
        "rskgt,rtkd->rskgd", new_probs, fresh_value_heads, preferred_element_type=jnp.float32
    )
    return mixed.astype(jnp.bfloat16).reshape(row_count, step_count, width)


def prefill_rows(states, length, norm_gain, w_query, w_key, w_value, w_out):
    row_count, resp_len, width = states.shape
    heads_kv = w_key.shape[1] // HD
    group_size = QH // KVH
    score_scale = 1.0 / math.sqrt(HD)
    states_f = states.astype(jnp.float32)
    mean_square = jnp.mean(states_f * states_f, axis=-1, keepdims=True)
    normed = (states_f * lax.rsqrt(mean_square + 1e-06) * norm_gain).astype(jnp.bfloat16)
    flat_rows = normed.reshape(row_count * resp_len, width)
    query_proj = jnp.dot(flat_rows, w_query, preferred_element_type=jnp.float32).astype(
        jnp.bfloat16
    )
    key_proj = jnp.dot(flat_rows, w_key, preferred_element_type=jnp.float32).astype(jnp.bfloat16)
    value_proj = jnp.dot(flat_rows, w_value, preferred_element_type=jnp.float32).astype(
        jnp.bfloat16
    )
    query_heads = query_proj.reshape(row_count, resp_len, heads_kv, group_size, HD)
    key_heads = key_proj.reshape(row_count, resp_len, heads_kv, HD)
    value_heads = value_proj.reshape(row_count, resp_len, heads_kv, HD)
    scores = (
        jnp.einsum("rqkgd,rpkd->rkgqp", query_heads, key_heads, preferred_element_type=jnp.float32)
        * score_scale
    )
    positions = jnp.arange(resp_len)
    causal = positions[None, :] <= positions[:, None]
    allowed = causal[None, :, :] & (positions[None, None, :] < length[:, None, None])
    scores = jnp.where(allowed[:, None, None], scores, -1e30)
    top_score = jnp.max(scores, axis=-1, keepdims=True)
    weights = jnp.exp(scores - top_score)
    pre_probs = (weights / jnp.sum(weights, axis=-1, keepdims=True)).astype(jnp.bfloat16)
    attended = jnp.einsum(
        "rkgqp,rpkd->rqkgd", pre_probs, value_heads, preferred_element_type=jnp.float32
    )
    attended = attended.astype(jnp.bfloat16).reshape(
        row_count * resp_len, heads_kv * group_size * HD
    )
    return jnp.dot(attended, w_out, preferred_element_type=jnp.float32)


def general_body(
    dest_slot,
    finished,
    lengths,
    cache_keys,
    cache_values,
    responses,
    dec_queries,
    new_keys,
    new_values,
    norm_gain,
    w_query,
    w_key,
    w_value,
    w_out,
):
    inst_count = lax.axis_size("inst")
    here_index = lax.axis_index("inst")
    row_count = finished.shape[0]
    slot_count = dest_slot.shape[0]
    per_target = max(2, 2 * row_count // inst_count)
    bucket_count = inst_count * per_target
    target = (dest_slot // row_count).reshape(inst_count, row_count)
    earlier = jnp.arange(row_count)[None, :] < jnp.arange(row_count)[:, None]
    same_target = target[:, :, None] == target[:, None, :]
    order_rank = jnp.sum(jnp.where(same_target & earlier[None], 1, 0), axis=2).astype(jnp.int32)
    bucket = (target * per_target + order_rank).reshape(slot_count)
    own_bucket = lax.dynamic_slice_in_dim(bucket, here_index * row_count, row_count)
    source = (
        jnp.zeros((slot_count,), jnp.int32)
        .at[dest_slot]
        .set(jnp.arange(slot_count, dtype=jnp.int32))
    )
    arrivals = lax.dynamic_slice_in_dim(source, here_index * row_count, row_count)
    incoming = arrivals // row_count * per_target + order_rank.reshape(slot_count)[arrivals]
    received = (
        lax.all_to_all(
            place_rows(responses, own_bucket, bucket_count),
            "inst",
            split_axis=0,
            concat_axis=0,
            tiled=True,
        ),
        lax.all_to_all(
            place_rows(finished, own_bucket, bucket_count),
            "inst",
            split_axis=0,
            concat_axis=0,
            tiled=True,
        ),
        lax.all_to_all(
            place_rows(lengths, own_bucket, bucket_count),
            "inst",
            split_axis=0,
            concat_axis=0,
            tiled=True,
        ),
    )
    slot_states = received[0][incoming]
    slot_done = received[1][incoming]
    slot_length = received[2][incoming]
    moved_caches = (
        lax.all_to_all(
            place_rows(cache_keys, own_bucket, bucket_count),
            "inst",
            split_axis=0,
            concat_axis=0,
            tiled=True,
        ),
        lax.all_to_all(
            place_rows(cache_values, own_bucket, bucket_count),
            "inst",
            split_axis=0,
            concat_axis=0,
            tiled=True,
        ),
    )
    decoded = decode_rows(
        dec_queries,
        new_keys,
        new_values,
        moved_caches[0][incoming],
        moved_caches[1][incoming],
        slot_length,
    )
    decoded = jnp.where(slot_done[:, None, None] == 0, decoded, jnp.zeros_like(decoded))
    states = lax.all_gather(slot_states, "tp", axis=2, tiled=True)
    partial_value = prefill_rows(states, slot_length, norm_gain, w_query, w_key, w_value, w_out)
    summed = lax.psum_scatter(
        partial_value.astype(jnp.bfloat16), "tp", scatter_dimension=1, tiled=True
    ).astype(jnp.float32)
    resp_len = states.shape[1]
    summed = summed.reshape(row_count, resp_len, -1)
    keep_mask = (jnp.arange(resp_len)[None, :] < slot_length[:, None]) & (slot_done[:, None] == 1)
    prefilled = jnp.where(keep_mask[:, :, None], summed, 0.0).astype(jnp.bfloat16)
    return (decoded, prefilled)


def body(*args):
    row_count = args[1].shape[0]
    inst_count = lax.axis_size("inst")
    two_groups = 2 * (2 * row_count // inst_count) == row_count and inst_count == 4
    if two_groups and lax.axis_size("tp") == 4:
        return two_shift_body(*args)
    return general_body(*args)


def solution(mesh):
    return jax.shard_map(
        body,
        mesh=mesh,
        in_specs=(
            P("rep"),
            P(("rep", "inst")),
            P(("rep", "inst")),
            P(("rep", "inst"), None, "tp"),
            P(("rep", "inst"), None, "tp"),
            P(("rep", "inst"), None, "tp"),
            P(("rep", "inst"), None, "tp"),
            P(("rep", "inst"), None, "tp"),
            P(("rep", "inst"), None, "tp"),
            P(),
            P(None, "tp"),
            P(None, "tp"),
            P(None, "tp"),
            P("tp", None),
        ),
        out_specs=(P(("rep", "inst"), None, "tp"), P(("rep", "inst"), None, "tp")),
        check_vma=False,
    )
```

```python
import math

import jax
import jax.numpy as jnp
from jax import lax
from jax.experimental import pallas as pl
from jax.experimental.pallas import tpu as pltpu
from jax.sharding import PartitionSpec as P

QH = 32
KVH = 8
HD = 128
PROMPT = 128


BLOCK = 64
TILE = 512
COST = 3
NEAR_SHARES = (320, 384)
FAR_SHARES = (256, 256, 192)
NEG = -1e30
CAPACITY = 704


def layer_kernel(
    base,
    part_ref,
    start_ref,
    own_ref,
    across_ref,
    beside_ref,
    earlier_ref,
    gain_ref,
    wq_ref,
    wk_ref,
    wv_ref,
    w_out,
    send_ref,
    keep_ref,
    later_ref,
    states,
    inverse,
    qkv,
    attended,
):
    tokens, width = own_ref.shape
    features = states.shape[1]
    q_width = w_out.shape[0]
    kv_width = wk_ref.shape[1]
    group_size = QH // KVH
    part = part_ref[0]

    def columns_of(block):
        return pl.ds(pl.multiple_of(block * width, 128), width)

    states[:, columns_of(part)] = own_ref[...]
    states[:, columns_of(part ^ 2)] = across_ref[...]
    states[:, columns_of(part ^ 1)] = beside_ref[:, :width]
    states[:, columns_of(part ^ 3)] = beside_ref[:, width:]
    qkv[:PROMPT, q_width:] = earlier_ref[...]

    def norm_rows(b, carry):
        rows = pl.ds(pl.multiple_of(b * BLOCK, BLOCK), BLOCK)
        total = jnp.zeros((BLOCK, 128), jnp.float32)
        for c in range(0, features, 128):
            value = states[rows, c : c + 128].astype(jnp.float32) * gain_ref[:, c : c + 128]
            total = total + value * value
        mean = jnp.sum(total, axis=1, keepdims=True) * (1.0 / features)
        inverse[rows, :] = jnp.broadcast_to(lax.rsqrt(mean + 1e-06), (BLOCK, 128))
        return carry

    lax.fori_loop(0, tokens // BLOCK, norm_rows, 0)
    def project(t, carry):
        columns = pl.ds(pl.multiple_of(t * TILE, TILE), TILE)
        product = jnp.dot(states[...], wq_ref[:, columns], preferred_element_type=jnp.float32)
        scale = inverse[...] * (math.log2(math.e) / math.sqrt(HD))
        scale = jnp.concatenate([scale] * (TILE // 128), axis=1)
        qkv[PROMPT:, columns] = (product * scale).astype(jnp.bfloat16)
        return carry

    lax.fori_loop(0, q_width // TILE, project, 0)
    scale = jnp.concatenate([inverse[...]] * (kv_width // 128), axis=1)
    for first, w_ref in ((q_width, wk_ref), (q_width + kv_width, wv_ref)):
        product = jnp.dot(states[...], w_ref[...], preferred_element_type=jnp.float32)
        qkv[PROMPT:, first : first + kv_width] = (product * scale).astype(jnp.bfloat16)

    shape = (BLOCK, BLOCK + PROMPT)

    def attend(b, carry):
        row = pl.multiple_of(b * BLOCK, BLOCK)
        query_pos = base + row + lax.broadcasted_iota(jnp.int32, shape, 0)
        key_pos = base + row - PROMPT + lax.broadcasted_iota(jnp.int32, shape, 1)
        token = base + row + lax.broadcasted_iota(jnp.int32, (BLOCK, 1), 0)
        start = jnp.zeros((BLOCK, 1), jnp.int32)
        for r in range(start_ref.shape[0]):
            begin = start_ref[r]
            start = jnp.where(token >= begin, jnp.maximum(start, begin), start)
        allowed = (key_pos >= start) & (key_pos <= query_pos)
        bias = jnp.where(allowed, 0.0, NEG)
        bias = jnp.concatenate([bias] * group_size, axis=0)
        query_rows = pl.ds(pl.multiple_of(row + PROMPT, BLOCK), BLOCK)
        key_rows = pl.ds(row, BLOCK + PROMPT)
        for head in range(kv_width // HD):
            columns = [(head * group_size + g) * HD for g in range(group_size)]
            queries = jnp.concatenate([qkv[query_rows, c : c + HD] for c in columns], axis=0)
            first = q_width + head * HD
            keys = qkv[key_rows, first : first + HD]
            values = qkv[key_rows, first + kv_width : first + kv_width + HD]
            scores = lax.dot_general(
                queries, keys, (((1,), (1,)), ((), ())), preferred_element_type=jnp.float32
            )
            scores = scores + bias
            weights = jnp.exp2(scores - jnp.max(scores, axis=-1, keepdims=True))
            values = jnp.concatenate([values, jnp.ones_like(values)], axis=1)
            mixed = jnp.dot(
                weights.astype(jnp.bfloat16), values, preferred_element_type=jnp.float32
            )
            mixed = (mixed[:, :HD] * (1.0 / mixed[:, HD:])).astype(jnp.bfloat16)
            for g, c in enumerate(columns):
                attended[pl.ds(row, BLOCK), c : c + HD] = mixed[g * BLOCK : (g + 1) * BLOCK]
        return carry

    lax.fori_loop(0, tokens // BLOCK, attend, 0)
    later_ref[...] = qkv[tokens:, q_width:]

    def out_block(place, carry):
        block = part ^ jnp.where(place == 0, 1, jnp.where(place == 1, 3, jnp.where(place == 2, 0, 2)))
        product = jnp.dot(
            attended[...], w_out[:, columns_of(block)], preferred_element_type=jnp.float32
        ).astype(jnp.bfloat16)

        @pl.when(place < 2)
        def _():
            send_ref[:, columns_of(place)] = product

        @pl.when(place >= 2)
        def _():
            keep_ref[:, columns_of(place - 2)] = product

        return carry

    lax.fori_loop(0, 4, out_block, 0)


def layer(base, part, row_start, own, other, beside, earlier, inverse_gain, weights):
    tokens, width = own.shape
    w_out = weights[3]
    q_width, features = w_out.shape
    kv_width = weights[1].shape[1]
    whole = pl.BlockSpec(memory_space=pltpu.VMEM)
    half = jax.ShapeDtypeStruct((tokens, 2 * width), jnp.bfloat16)
    return pl.pallas_call(
        lambda *refs: layer_kernel(base, *refs),
        in_specs=[pl.BlockSpec(memory_space=pltpu.SMEM)] * 2 + [whole] * 9,
        out_specs=[whole] * 3,
        out_shape=[half, half, jax.ShapeDtypeStruct((PROMPT, 2 * kv_width), jnp.bfloat16)],
        scratch_shapes=[
            pltpu.VMEM((tokens, features), jnp.bfloat16),
            pltpu.VMEM((tokens, 128), jnp.float32),
            pltpu.VMEM((tokens + PROMPT, q_width + 2 * kv_width), jnp.bfloat16),
            pltpu.VMEM((tokens, q_width), jnp.bfloat16),
        ],
        compiler_params=pltpu.CompilerParams(vmem_limit_bytes=28 * 2**20),
        cost_estimate=pl.CostEstimate(
            flops=COST * 2 * tokens * features * (2 * q_width + 2 * kv_width),
            bytes_accessed=1024,
            transcendentals=0,
        ),
        name="prefill_layer",
    )(part[None], row_start, own, other, beside, earlier, inverse_gain, *weights)


def unpack_kernel(cuts, used_ref, offset_ref, *refs):
    pieces, out_ref, held = refs[:-2], refs[-2], refs[-1]
    step = pl.program_id(0)

    @pl.when(step == 0)
    def _():
        for low, piece in zip(cuts, pieces):
            held[low : low + piece.shape[0], :] = piece[...]
        end = cuts[-1] + pieces[-1].shape[0]
        held[end:, :] = jnp.zeros((held.shape[0] - end, held.shape[1]), held.dtype)

    per_step, resp_len = out_ref.shape[:2]
    token = lax.broadcasted_iota(jnp.int32, (resp_len, 2 * resp_len), 0)
    place = lax.broadcasted_iota(jnp.int32, (resp_len, 2 * resp_len), 1)
    for k in range(per_step):
        offset = offset_ref[step * per_step + k]
        first = pl.multiple_of(offset // 16 * 16, 16)
        window = held[pl.ds(first, 2 * resp_len), :]
        mask = (place == token + (offset - first)) & (token < used_ref[step * per_step + k])
        mask = jnp.where(mask, 1.0, 0.0).astype(jnp.bfloat16)
        out_ref[k] = jnp.dot(mask, window, preferred_element_type=jnp.float32).astype(jnp.bfloat16)


def unpack(used, offset, pieces, cuts, resp_len):
    slots, width = used.shape[0], pieces[0].shape[1]
    per_step = 2 if slots % 2 == 0 else 1
    full = lambda piece: pl.BlockSpec(piece.shape, lambda s, *_: (0, 0))
    return pl.pallas_call(
        lambda *refs: unpack_kernel(cuts, *refs),
        grid_spec=pltpu.PrefetchScalarGridSpec(
            num_scalar_prefetch=2,
            grid=(slots // per_step,),
            in_specs=[full(piece) for piece in pieces],
            out_specs=pl.BlockSpec((per_step, resp_len, width), lambda s, *_: (s, 0, 0)),
            scratch_shapes=[pltpu.VMEM((cuts[-1] + pieces[-1].shape[0] + 2 * resp_len, width), jnp.bfloat16)],
        ),
        out_shape=jax.ShapeDtypeStruct((slots, resp_len, width), jnp.bfloat16),
        compiler_params=pltpu.CompilerParams(vmem_limit_bytes=24 * 2**20),
        name="unpack_slots",
    )(used, offset, *pieces)


def decode_kernel(length_ref, active_ref, fresh_ref, key_ref, value_ref, out_ref):
    row = pl.program_id(0)
    group, kv_width = QH // KVH, key_ref.shape[2]
    q_width = group * kv_width
    steps = out_ref.shape[2] // q_width
    stride = q_width + 2 * kv_width

    @pl.when(active_ref[row] == 0)
    def _():
        out_ref[...] = jnp.zeros_like(out_ref)

    @pl.when(active_ref[row] != 0)
    def _():
        scale = 1.0 / math.sqrt(HD)
        valid = PROMPT + length_ref[row]
        keys, values = key_ref[0], value_ref[0]
        nums = (((1,), (1,)), ((), ()))

        def stacked(starts):
            rows = [fresh_ref[0, :, start : start + HD] for start in starts]
            if len(rows) < 8:
                rows.append(jnp.zeros((8 - len(rows), HD), jnp.float32))
            return jnp.concatenate(rows, axis=0).astype(jnp.bfloat16)

        for head in range(kv_width // HD):
            order = [(t, head * group + g) for t in range(steps) for g in range(group)]
            queries = stacked([t * stride + h * HD for t, h in order])
            first = q_width + head * HD
            new_keys = stacked([t * stride + first for t in range(steps)])
            new_values = stacked([t * stride + first + kv_width for t in range(steps)])
            lanes = slice(head * HD, (head + 1) * HD)
            old = lax.dot_general(queries, keys[:, lanes], nums, preferred_element_type=jnp.float32)
            new = lax.dot_general(queries, new_keys, nums, preferred_element_type=jnp.float32)
            position = lax.broadcasted_iota(jnp.int32, old.shape, 1)
            old = jnp.where(position < valid, old * scale, NEG)
            step = lax.broadcasted_iota(jnp.int32, new.shape, 0) // group
            new = jnp.where(lax.broadcasted_iota(jnp.int32, new.shape, 1) <= step, new * scale, NEG)
            top = jnp.maximum(
                jnp.max(old, axis=-1, keepdims=True), jnp.max(new, axis=-1, keepdims=True)
            )
            old_weights, new_weights = jnp.exp(old - top), jnp.exp(new - top)
            total = jnp.sum(old_weights, axis=-1, keepdims=True) + jnp.sum(
                new_weights, axis=-1, keepdims=True
            )
            mixed = jnp.dot(
                (old_weights / total).astype(jnp.bfloat16),
                values[:, lanes],
                preferred_element_type=jnp.float32,
            ) + jnp.dot(
                (new_weights / total).astype(jnp.bfloat16),
                new_values,
                preferred_element_type=jnp.float32,
            )
            for k, (t, h) in enumerate(order):
                out_ref[0, :, t * q_width + h * HD : t * q_width + (h + 1) * HD] = mixed[k : k + 1]


def decode_here(length, active, fresh, cache_keys, cache_values, steps):
    rows, cache_len, kv_width = cache_keys.shape
    q_width = QH // KVH * kv_width
    cache = pl.BlockSpec((1, cache_len, kv_width), lambda r, *_: (r, 0, 0))
    out = pl.pallas_call(
        decode_kernel,
        grid_spec=pltpu.PrefetchScalarGridSpec(
            num_scalar_prefetch=2,
            grid=(rows,),
            in_specs=[
                pl.BlockSpec((1, 1, fresh.shape[1]), lambda r, *_: (r, 0, 0)),
                cache,
                cache,
            ],
            out_specs=pl.BlockSpec((1, 1, steps * q_width), lambda r, *_: (r, 0, 0)),
        ),
        out_shape=jax.ShapeDtypeStruct((rows, 1, steps * q_width), jnp.float32),
        compiler_params=pltpu.CompilerParams(vmem_limit_bytes=16 * 2**20),
        cost_estimate=pl.CostEstimate(
            flops=4 * rows * cache_len * steps * q_width,
            bytes_accessed=8 * rows * cache_len * kv_width,
            transcendentals=0,
        ),
        name="decode_attention",
    )(length, active, fresh[:, None], cache_keys, cache_values)
    return out[:, 0].astype(jnp.bfloat16)


def pick(mask, values):
    return jnp.dot(
        mask.astype(jnp.bfloat16), values, preferred_element_type=jnp.float32
    ).astype(jnp.bfloat16)


def two_shift_body(
    dest_slot,
    finished,
    lengths,
    cache_keys,
    cache_values,
    responses,
    dec_queries,
    new_keys,
    new_values,
    norm_gain,
    w_query,
    w_key,
    w_value,
    w_out,
):
    count = lax.axis_size("inst")
    here = lax.axis_index("inst")
    part = lax.axis_index("tp")
    tp = lax.axis_size("tp")
    reps = lax.axis_size("rep")
    rows, resp_len, width = responses.shape
    steps = dec_queries.shape[1]
    near, far = 1, count // 2
    cap = rows // 2
    full_cap = cap * resp_len

    def along(value, shift):
        return lax.ppermute(value, "inst", [(i, (i + shift) % count) for i in range(count)])

    def across(value):
        return lax.ppermute(value, "tp", [(i, i ^ 2) for i in range(tp)])

    def beside(value):
        return lax.ppermute(value, "tp", [(i, i ^ 1) for i in range(tp)])

    def ordered(value, *after):
        return lax.optimization_barrier((value,) + after)[0]

    slots = dest_slot.reshape(count, rows)
    shift = (slots // rows - jnp.arange(count)[:, None]) % count
    earlier = jnp.arange(rows)[None, :] < jnp.arange(rows)[:, None]

    def at(table, shift_back):
        return lax.dynamic_index_in_dim(table, (here - shift_back) % count, 0, keepdims=False)

    def rank_of(own_shift):
        same = own_shift[:, None] == own_shift[None, :]
        return jnp.sum((same & earlier).astype(jnp.int32), axis=1)

    own_slots, own_shift = at(slots, 0), at(shift, 0)
    own_rank = rank_of(own_shift)

    def layout(length, done, row_shift, which):
        used = jnp.where((row_shift == which) & (done == 1), length, 0)
        offset = jnp.sum(jnp.where(earlier, used[None, :], 0), axis=1)
        return used, offset, jnp.sum(used)

    def places(used, offset):
        inside = jnp.arange(resp_len)[None, :] < used[:, None]
        return jnp.where(inside, offset[:, None] + jnp.arange(resp_len)[None, :], -1)

    def starts(used, offset):
        return jnp.where(used > 0, offset, 2 * full_cap)

    used_near, offset_near, total_near = layout(lengths, finished, own_shift, near)
    used_far, offset_far, total_far = layout(lengths, finished, own_shift, far)
    place_near = places(used_near, offset_near).reshape(1, rows * resp_len)
    place_far = places(used_far, offset_far).reshape(1, rows * resp_len)
    flat = responses.reshape(rows * resp_len, width)
    own_gain = lax.dynamic_slice_in_dim(norm_gain, part * width, width)


    def packed(place, low, high):
        token = jnp.arange(low, high, dtype=jnp.int32)[:, None]
        chosen = jnp.dot(
            (token == place).astype(jnp.bfloat16), flat, preferred_element_type=jnp.float32
        )
        return (chosen * own_gain).astype(jnp.bfloat16)

    fresh = jnp.concatenate([dec_queries, new_keys, new_values], axis=2)
    fresh = fresh.reshape(rows, -1)

    def slot_of(shift_back, row_rank, row_shift, which):
        source_slots = at(slots, shift_back)
        source_shift = at(shift, shift_back)
        local = jnp.where(source_shift == which, source_slots - here * rows, -1)
        hit = local[None, :] == jnp.arange(rows)[:, None]
        return hit

    def rank_mask(row_shift, row_rank, which):
        member = (row_shift == which)[:, None]
        return member & (row_rank[:, None] == jnp.arange(cap)[None, :])

    near_shift, far_shift = at(shift, near), at(shift, far)
    near_rank, far_rank = rank_of(near_shift), rank_of(far_shift)
    near_hit = slot_of(near, near_rank, near_shift, near)
    far_hit = slot_of(far, far_rank, far_shift, far)
    near_slot = jnp.any(near_hit[:, :, None] & rank_mask(near_shift, near_rank, near)[None], axis=1)
    far_slot = jnp.any(far_hit[:, :, None] & rank_mask(far_shift, far_rank, far)[None], axis=1)
    most = jnp.maximum(total_near, total_far)
    notes = jnp.concatenate(
        [lengths, finished, jnp.stack([most // resp_len, most % resp_len])]
    ).astype(jnp.bfloat16)

    notes = jnp.pad(notes, (0, -notes.shape[0] % HD))[None]

    def noted(values):
        line = jnp.pad(notes, ((0, 0), (0, values.shape[1] - notes.shape[1])))
        return jnp.concatenate([values, line], axis=0)

    def read(values):
        line = values[-1, : 2 * rows + 2].astype(jnp.int32)
        return line[:rows], line[rows : 2 * rows], line[2 * rows] * resp_len + line[2 * rows + 1]

    own_near = rank_mask(own_shift, own_rank, near)
    own_far = rank_mask(own_shift, own_rank, far)
    away_near, away_far = noted(pick(near_slot.T, fresh)), noted(pick(far_slot.T, fresh))
    back_near, back_far = along(away_near, -near), along(away_far, -far)
    from_near, from_far, from_third = read(along(notes, near)), read(back_far), read(back_near)
    flat = ordered(flat, away_near, away_far)
    far_states = packed(place_far, 0, full_cap)
    far_first = far_states[: FAR_SHARES[0]]
    flat = ordered(flat, far_first)
    near_states = packed(place_near, 0, full_cap)
    own_group = jnp.concatenate([own_near, own_far], axis=1)
    own_fresh = pick(own_group, jnp.concatenate([back_near[:cap], back_far[:cap]], axis=0))
    inverse_gain = (1.0 / norm_gain)[None]

    start_near = starts(used_near, offset_near)

    def arrived(meta_came, row_shift, which):
        return layout(meta_came[0], meta_came[1], row_shift, which)

    def by_slot(hit, values):
        return jnp.sum(jnp.where(hit, values[None], 0), axis=1)

    kv_width = w_key.shape[1] + w_value.shape[1]

    capacity = min(CAPACITY, full_cap)

    def cut(shares):
        marks = [0]
        for k in range(1, len(shares)):
            marks.append(round(capacity * sum(shares[:k]) / sum(shares) / BLOCK) * BLOCK)
        return marks + [capacity]

    none = jnp.zeros((PROMPT, kv_width), jnp.bfloat16)
    weights = (w_query, w_key, w_value, w_out)
    near_cuts, far_cuts = cut(NEAR_SHARES), cut(FAR_SHARES)
    near_parts = [near_states[a:b] for a, b in zip(near_cuts, near_cuts[1:])]
    near_others = [across(piece) for piece in near_parts]
    far_parts = [far_states[a:b] for a, b in zip(far_cuts, far_cuts[1:])]
    far_parts[0] = along(far_first, far)
    arrived_last = far_parts[0]
    for came in (from_near, from_far, from_third):
        most = jnp.maximum(most, came[2])
    for k in range(1, reps):
        pairs = [(i, (i + k) % reps) for i in range(reps)]
        most = jnp.maximum(most, lax.ppermute(most, "rep", pairs))
    used_a, offset_a, _ = arrived(from_near, near_shift, near)
    used_b, offset_b, _ = arrived(from_far, far_shift, far)
    start_far = starts(used_b, offset_b)
    decoded = decode_here(
        lengths, 1 - finished, own_fresh.astype(jnp.float32), cache_keys, cache_values, steps
    )
    came_near = along(pick(own_near.T, decoded), near)
    came_far = along(pick(own_far.T, decoded), far)
    lows = near_cuts[:-1] + far_cuts[:-1]
    first_far, last = len(near_parts), len(lows) - 1
    owns = near_parts + far_parts
    others, boths, cames = list(near_others), [], []
    sent, kept, crossed, chips, turned, done = [], [], [], [], [], []

    def after_kernel(value, c):
        return ordered(value, sent[c]) if 0 <= c < len(sent) else value

    last_sent = []

    def fetch(c):
        if first_far < c <= last:
            gone = owns[c - 1] if c - 1 > first_far else arrived_last
            owns[c] = along(ordered(owns[c], after_kernel(gone, c - 4)), far)

    def meet(c):
        if c == len(others):
            others.append(across(after_kernel(owns[c], c - 3)))
        other = after_kernel(others[c], c - 2)
        own = after_kernel(owns[c], c - 2)
        boths.append(jnp.concatenate([own, other], axis=1))
        cames.append(beside(boths[c]))

    def add(c):
        chips.append(after_kernel(crossed[c], c + 1))
        both = kept[c][:, width:].astype(jnp.float32) + chips[c][:, width:].astype(jnp.float32)
        both = both.astype(jnp.bfloat16)
        turned.append(across(both))
        return both

    def finish(c):
        got = after_kernel(turned[c], c + 3)
        if last_sent and first_far <= c < last:
            got = ordered(got, last_sent[0])
        got = got.astype(jnp.float32)
        both = kept[c][:, :width].astype(jnp.float32) + chips[c][:, :width].astype(jnp.float32)
        total = (both + got).astype(jnp.bfloat16)
        done.append(along(total, near) if c < first_far else total)
        return total

    fetch(first_far + 1)
    meet(0)
    tail = none
    for c, low in enumerate(lows):
        before = [boths[0], decoded, most] if c == 0 else [came_near, came_far] if c == 1 else []
        fetch(c + 3 if c + 3 > first_far + 1 else -1)
        if c < last:
            meet(c + 1)
            before.append(boths[c + 1])
        if c >= 2:
            before.append(add(c - 2))
        if c == 4:
            before.append(finish(0))
        if c == first_far:
            near_tail = tail
            tail = ordered(none, tail)
        tail = ordered(tail, *before)
        high = low + owns[c].shape[0]
        row_start = start_near if c < first_far else start_far
        send, keep, tail = layer(
            low,
            part,
            row_start,
            owns[c],
            others[c],
            cames[c],
            tail,
            inverse_gain,
            weights,
        )
        sent.append(send)
        kept.append(keep)
        crossed.append(beside(send))
    for c in range(len(chips), last):
        add(c)
    while len(done) < first_far:
        kept[last] = ordered(kept[last], finish(len(done)), done[0])
    last_sent.append(add(last))
    for c in range(len(done), last + 1):
        finish(c)
    near_done, far_done = done[:first_far], done[first_far:]

    def overflow(near_x, far_x, near_kv, far_kv):
        def run(low, own, kv, row_start):
            other = across(own)
            came = beside(jnp.concatenate([own, other], axis=1))
            send, keep, _ = layer(
                low, part, row_start, own, other, came, kv, inverse_gain, weights
            )
            chip = keep.astype(jnp.float32) + beside(send).astype(jnp.float32)
            got = across(chip[:, width:].astype(jnp.bfloat16))
            return (chip[:, :width] + got.astype(jnp.float32)).astype(jnp.bfloat16)

        near_more = along(run(capacity, near_x, near_kv, start_near), near)
        far_more = run(capacity, along(far_x, far), far_kv, start_far)
        return near_more, far_more

    def nothing(near_x, far_x, near_kv, far_kv):
        return jnp.zeros_like(near_x), jnp.zeros_like(far_x)

    if capacity < full_cap:
        near_more, far_more = lax.cond(
            most > capacity,
            overflow,
            nothing,
            near_states[capacity:],
            far_states[capacity:],
            near_tail,
            tail,
        )
        near_done, far_done = near_done + [near_more], far_done + [far_more]
        near_cuts, far_cuts = near_cuts + [full_cap], far_cuts + [full_cap]
    cuts = near_cuts[:-1] + [full_cap + cut_ for cut_ in far_cuts[:-1]]
    near_used, far_used = by_slot(near_hit, used_a), by_slot(far_hit, used_b)
    near_offset, far_offset = by_slot(near_hit, offset_a), by_slot(far_hit, offset_b)
    offset = near_offset + jnp.where(far_used > 0, far_offset + full_cap, 0)
    prefilled = unpack(near_used + far_used, offset, near_done + far_done, cuts, resp_len)
    active_slot = jnp.concatenate([near_slot, far_slot], axis=1)
    decoded = pick(active_slot, jnp.concatenate([came_near, came_far], axis=0))
    return decoded.reshape(rows, steps, -1), prefilled


def place_rows(values, index, count):
    buffer = jnp.zeros((count,) + values.shape[1:], values.dtype)
    return buffer.at[index].set(values)


def decode_rows(queries, fresh_keys, fresh_values, old_keys, old_values, length):
    row_count, step_count, width = queries.shape
    heads_kv = old_keys.shape[2] // HD
    group_size = QH // KVH
    cache_len = old_keys.shape[1]
    score_scale = 1.0 / math.sqrt(HD)
    query_heads = queries.reshape(row_count, step_count, heads_kv, group_size, HD)
    key_heads = old_keys.reshape(row_count, cache_len, heads_kv, HD)
    value_heads = old_values.reshape(row_count, cache_len, heads_kv, HD)
    fresh_key_heads = fresh_keys.reshape(row_count, step_count, heads_kv, HD)
    fresh_value_heads = fresh_values.reshape(row_count, step_count, heads_kv, HD)
    old_scores = (
        jnp.einsum("rskgd,rpkd->rskgp", query_heads, key_heads, preferred_element_type=jnp.float32)
        * score_scale
    )
    new_scores = (
        jnp.einsum(
            "rskgd,rtkd->rskgt", query_heads, fresh_key_heads, preferred_element_type=jnp.float32
        )
        * score_scale
    )
    old_valid = jnp.arange(cache_len)[None, :] < PROMPT + length[:, None]
    step_index = jnp.arange(step_count)
    new_valid = step_index[None, :] <= step_index[:, None]
    old_scores = jnp.where(old_valid[:, None, None, None, :], old_scores, -1e30)
    new_scores = jnp.where(new_valid[None, :, None, None, :], new_scores, -1e30)
    top_score = jnp.maximum(
        jnp.max(old_scores, axis=-1, keepdims=True), jnp.max(new_scores, axis=-1, keepdims=True)
    )
    old_weights = jnp.exp(old_scores - top_score)
    new_weights = jnp.exp(new_scores - top_score)
    totals = jnp.sum(old_weights, axis=-1, keepdims=True) + jnp.sum(
        new_weights, axis=-1, keepdims=True
    )
    old_probs = (old_weights / totals).astype(jnp.bfloat16)
    new_probs = (new_weights / totals).astype(jnp.bfloat16)
    mixed = jnp.einsum(
        "rskgp,rpkd->rskgd", old_probs, value_heads, preferred_element_type=jnp.float32
    )
    mixed = mixed + jnp.einsum(
        "rskgt,rtkd->rskgd", new_probs, fresh_value_heads, preferred_element_type=jnp.float32
    )
    return mixed.astype(jnp.bfloat16).reshape(row_count, step_count, width)


def prefill_rows(states, length, norm_gain, w_query, w_key, w_value, w_out):
    row_count, resp_len, width = states.shape
    heads_kv = w_key.shape[1] // HD
    group_size = QH // KVH
    score_scale = 1.0 / math.sqrt(HD)
    states_f = states.astype(jnp.float32)
    mean_square = jnp.mean(states_f * states_f, axis=-1, keepdims=True)
    normed = (states_f * lax.rsqrt(mean_square + 1e-06) * norm_gain).astype(jnp.bfloat16)
    flat_rows = normed.reshape(row_count * resp_len, width)
    query_proj = jnp.dot(flat_rows, w_query, preferred_element_type=jnp.float32).astype(
        jnp.bfloat16
    )
    key_proj = jnp.dot(flat_rows, w_key, preferred_element_type=jnp.float32).astype(jnp.bfloat16)
    value_proj = jnp.dot(flat_rows, w_value, preferred_element_type=jnp.float32).astype(
        jnp.bfloat16
    )
    query_heads = query_proj.reshape(row_count, resp_len, heads_kv, group_size, HD)
    key_heads = key_proj.reshape(row_count, resp_len, heads_kv, HD)
    value_heads = value_proj.reshape(row_count, resp_len, heads_kv, HD)
    scores = (
        jnp.einsum("rqkgd,rpkd->rkgqp", query_heads, key_heads, preferred_element_type=jnp.float32)
        * score_scale
    )
    positions = jnp.arange(resp_len)
    causal = positions[None, :] <= positions[:, None]
    allowed = causal[None, :, :] & (positions[None, None, :] < length[:, None, None])
    scores = jnp.where(allowed[:, None, None], scores, -1e30)
    top_score = jnp.max(scores, axis=-1, keepdims=True)
    weights = jnp.exp(scores - top_score)
    pre_probs = (weights / jnp.sum(weights, axis=-1, keepdims=True)).astype(jnp.bfloat16)
    attended = jnp.einsum(
        "rkgqp,rpkd->rqkgd", pre_probs, value_heads, preferred_element_type=jnp.float32
    )
    attended = attended.astype(jnp.bfloat16).reshape(
        row_count * resp_len, heads_kv * group_size * HD
    )
    return jnp.dot(attended, w_out, preferred_element_type=jnp.float32)


def general_body(
    dest_slot,
    finished,
    lengths,
    cache_keys,
    cache_values,
    responses,
    dec_queries,
    new_keys,
    new_values,
    norm_gain,
    w_query,
    w_key,
    w_value,
    w_out,
):
    inst_count = lax.axis_size("inst")
    here_index = lax.axis_index("inst")
    row_count = finished.shape[0]
    slot_count = dest_slot.shape[0]
    per_target = max(2, 2 * row_count // inst_count)
    bucket_count = inst_count * per_target
    target = (dest_slot // row_count).reshape(inst_count, row_count)
    earlier = jnp.arange(row_count)[None, :] < jnp.arange(row_count)[:, None]
    same_target = target[:, :, None] == target[:, None, :]
    order_rank = jnp.sum(jnp.where(same_target & earlier[None], 1, 0), axis=2).astype(jnp.int32)
    bucket = (target * per_target + order_rank).reshape(slot_count)
    own_bucket = lax.dynamic_slice_in_dim(bucket, here_index * row_count, row_count)
    source = (
        jnp.zeros((slot_count,), jnp.int32)
        .at[dest_slot]
        .set(jnp.arange(slot_count, dtype=jnp.int32))
    )
    arrivals = lax.dynamic_slice_in_dim(source, here_index * row_count, row_count)
    incoming = arrivals // row_count * per_target + order_rank.reshape(slot_count)[arrivals]
    received = (
        lax.all_to_all(
            place_rows(responses, own_bucket, bucket_count),
            "inst",
            split_axis=0,
            concat_axis=0,
            tiled=True,
        ),
        lax.all_to_all(
            place_rows(finished, own_bucket, bucket_count),
            "inst",
            split_axis=0,
            concat_axis=0,
            tiled=True,
        ),
        lax.all_to_all(
            place_rows(lengths, own_bucket, bucket_count),
            "inst",
            split_axis=0,
            concat_axis=0,
            tiled=True,
        ),
    )
    slot_states = received[0][incoming]
    slot_done = received[1][incoming]
    slot_length = received[2][incoming]
    moved_caches = (
        lax.all_to_all(
            place_rows(cache_keys, own_bucket, bucket_count),
            "inst",
            split_axis=0,
            concat_axis=0,
            tiled=True,
        ),
        lax.all_to_all(
            place_rows(cache_values, own_bucket, bucket_count),
            "inst",
            split_axis=0,
            concat_axis=0,
            tiled=True,
        ),
    )
    decoded = decode_rows(
        dec_queries,
        new_keys,
        new_values,
        moved_caches[0][incoming],
        moved_caches[1][incoming],
        slot_length,
    )
    decoded = jnp.where(slot_done[:, None, None] == 0, decoded, jnp.zeros_like(decoded))
    states = lax.all_gather(slot_states, "tp", axis=2, tiled=True)
    partial_value = prefill_rows(states, slot_length, norm_gain, w_query, w_key, w_value, w_out)
    summed = lax.psum_scatter(
        partial_value.astype(jnp.bfloat16), "tp", scatter_dimension=1, tiled=True
    ).astype(jnp.float32)
    resp_len = states.shape[1]
    summed = summed.reshape(row_count, resp_len, -1)
    keep_mask = (jnp.arange(resp_len)[None, :] < slot_length[:, None]) & (slot_done[:, None] == 1)
    prefilled = jnp.where(keep_mask[:, :, None], summed, 0.0).astype(jnp.bfloat16)
    return (decoded, prefilled)


def body(*args):
    row_count = args[1].shape[0]
    inst_count = lax.axis_size("inst")
    two_groups = 2 * (2 * row_count // inst_count) == row_count and inst_count == 4
    if two_groups and lax.axis_size("tp") == 4:
        return two_shift_body(*args)
    return general_body(*args)


def solution(mesh):
    return jax.shard_map(
        body,
        mesh=mesh,
        in_specs=(
            P("rep"),
            P(("rep", "inst")),
            P(("rep", "inst")),
            P(("rep", "inst"), None, "tp"),
            P(("rep", "inst"), None, "tp"),
            P(("rep", "inst"), None, "tp"),
            P(("rep", "inst"), None, "tp"),
            P(("rep", "inst"), None, "tp"),
            P(("rep", "inst"), None, "tp"),
            P(),
            P(None, "tp"),
            P(None, "tp"),
            P(None, "tp"),
            P("tp", None),
        ),
        out_specs=(P(("rep", "inst"), None, "tp"), P(("rep", "inst"), None, "tp")),
        check_vma=False,
    )
```
